128 devices in a mesh: row: 8 (over y, core), col: 16 (over z, x).
Axes of the slice: x: 4, y: 4, z: 4, core: 2. Of those that a mesh axis runs over, the one named last changes fastest.
Arguments:
- sigma_top: float32 [6144, 6144], P('row', 'col')
- factor_cross: float32 [6144, 6144], P('row', 'col'), may hold values from -0.078125 to 0.078125
- factor_inverse: float32 [6144, 6144], P('row', 'col')
- block_inverse: float32 [6144, 6144], P('row', 'col')
- ancestors: int32 [12], replicated, may hold values from 0 to 23, as said below
Outputs:
- sigma_cross: float32 [6144, 6144], P('row', 'col')
- sigma_child: float32 [6144, 6144], P('row', 'col')
The draws below stay inside these ranges and needn't reach their ends.
Inputs may be any that keep to these rules, and one draw needn't show every extreme that they name: `ancestors`: 12 distinct block numbers; block 0 and block 23 are always among them.
All inputs are finite; a program needn't handle non-finite values.
Results may differ from the reference program's by a relative error of at most 0.000078.
Values sent between devices are 32-bit elements; how exact they have to be, the bound alone decides.
No kernel may reach another device: no remote copies, remote signals or barrier semaphores. Data moves between devices by JAX's collectives and lax.ppermute only.
A program may use at most 128 MiB of HBM per device.

```python
import math
import jax
import jax.numpy as jnp
from jax import lax

ORDER = 6144
BLK = 256
NB = 24
NANC = 12


def symmetric_from(noise, key, lowest, highest):
    off_part = (noise + noise.T) * (0.70710678 / math.sqrt(ORDER))
    diagonal = jnp.exp(jax.random.uniform(key, (ORDER,), jnp.float32, math.log(lowest), math.log(highest)))
    return off_part + jnp.diag(diagonal)


def draw_sigma_top(key, part):
    first, second = jax.random.split(jax.random.fold_in(key, 11))
    noise = jax.random.normal(first, (ORDER, ORDER), jnp.float32)
    return symmetric_from(noise, second, 2.0, 6.0)


def draw_block_inverse(key, part):
    first, second = jax.random.split(jax.random.fold_in(key, 23))
    noise = jax.random.normal(first, (ORDER, ORDER), jnp.float32)
    return symmetric_from(noise, second, 1.0, 4.0)


def draw_factor_inverse(key, part):
    first, second = jax.random.split(jax.random.fold_in(key, 37))
    noise = jax.random.normal(first, (ORDER, ORDER), jnp.float32)
    diagonal = jnp.exp(jax.random.uniform(second, (ORDER,), jnp.float32, math.log(0.5), math.log(2.0)))
    return jnp.tril(noise, -1) * (1.0 / math.sqrt(ORDER)) + jnp.diag(diagonal)


def draw_ancestors(key, part):
    shuffled = jax.random.permutation(jax.random.fold_in(key, 53), NB - 2).astype(jnp.int32) + 1
    ends = jnp.array([0, NB - 1], dtype=jnp.int32)
    return jnp.concatenate([ends, shuffled[:NANC - 2]]).astype(jnp.int32)


def block_levels(rng, extent, cuts, smallest, largest):
    level, own = 1.0, jax.random.fold_in(rng, 6)
    for axis_at, blocks in cuts:
        draws = jnp.exp(jax.random.uniform(jax.random.fold_in(own, axis_at), (blocks,), jnp.float32, smallest / len(cuts), largest / len(cuts)))
        level = level * jnp.repeat(draws, extent[axis_at] // blocks).reshape([-1 if axis == axis_at else 1 for axis in range(len(extent))])
    return level


def bell_draw(rng, dims, spread, bound, cuts=(), kind=jnp.bfloat16):
    values = jax.random.normal(rng, dims, jnp.float32) * spread
    if len(cuts) > 0:
        values = block_levels(rng, dims, cuts, -0.22, 0.18) * values
    return jnp.clip(values, min=-bound, max=bound).astype(kind)


def setup_inputs(seed: int = 0) -> dict:
    streams_of = jax.random.split(jax.random.key(seed), 6)
    sigma_top = draw_sigma_top(jax.random.fold_in(streams_of[5], 71), 0)
    factor_cross = bell_draw(streams_of[1], (ORDER, ORDER), ORDER ** -0.5, 0.078125, ((0, 8), (1, 16)), jnp.float32)
    factor_inverse = draw_factor_inverse(jax.random.fold_in(streams_of[5], 71), 0)
    block_inverse = draw_block_inverse(jax.random.fold_in(streams_of[5], 71), 0)
    ancestors = draw_ancestors(jax.random.fold_in(streams_of[5], 71), 0)
    return dict(sigma_top=sigma_top, factor_cross=factor_cross, factor_inverse=factor_inverse, block_inverse=block_inverse, ancestors=ancestors)


def reference(sigma_top, factor_cross, factor_inverse, block_inverse, ancestors):
    blocks = jnp.arange(ORDER, dtype=jnp.int32) // BLK
    living = jnp.any(blocks[:, None] == ancestors[None, :], axis=1)
    masked = jnp.where(living[:, None], factor_cross, jnp.float32(0.0))
    update = jnp.dot(masked, factor_inverse, precision=lax.Precision.HIGHEST, preferred_element_type=jnp.float32)
    product = jnp.dot(sigma_top, update, precision=lax.Precision.HIGHEST, preferred_element_type=jnp.float32)
    sigma_cross = jnp.where(living[:, None], -product, jnp.float32(0.0))
    correction = jnp.dot(update.T, sigma_cross, precision=lax.Precision.HIGHEST, preferred_element_type=jnp.float32)
    sigma_child = block_inverse - correction
    return sigma_cross, sigma_child
```

```python
import jax
import jax.numpy as jnp
import numpy as np
from jax import lax
from jax.sharding import Mesh, PartitionSpec as P

NB = 24
NANC = 12
ROW = ("y", "core")
COL = ("z", "x")
ALL = ("y", "core", "z", "x")


def shift(x, axis, n, k):
    return lax.ppermute(x, axis, [(i, (i + k) % n) for i in range(n)])


def gather_rows(x):
    y, core = lax.axis_index("y"), lax.axis_index("core")
    half = x.shape[0] // 2
    left = shift(x, "y", 4, 1)
    right = shift(x, "y", 4, -1)
    far = jnp.concatenate([shift(left[:half], "y", 4, 1), shift(right[half:], "y", 4, -1)])
    mine = [x, left, right, far]
    at = [y, (y + 3) % 4, (y + 1) % 4, (y + 2) % 4]
    out = [(2 * a + core, t) for a, t in zip(at, mine)]
    out += [(2 * a + 1 - core, shift(t, "core", 2, 1)) for a, t in zip(at, mine)]
    return out


def spread(x):
    h, w = x.shape
    sub = h // 24
    return lax.all_to_all(x.reshape(3, 8, sub, w), ROW, 1, 0, tiled=True).reshape(NB, sub, w)


def pick(x, ancestors):
    return jnp.concatenate([lax.dynamic_slice_in_dim(x, ancestors[i], 1, 0) for i in range(NANC)])


def dot(a, b, dims):
    return lax.dot_general(a, b, (dims, ((), ())), precision=lax.Precision.HIGH, preferred_element_type=jnp.float32)


def per_device(sigma_top, factor_cross, factor_inverse, block_inverse, ancestors):
    h, w = sigma_top.shape
    sub = h // 24
    part = NANC * sub

    f = pick(spread(factor_cross), ancestors).reshape(part, w)
    f_all = lax.all_gather(f, COL, axis=1, tiled=True)
    strip = jnp.zeros((8 * h, w), jnp.float32)
    for r, t in gather_rows(factor_inverse):
        strip = lax.dynamic_update_slice(strip, t, (r * h, 0))
    s = pick(spread(sigma_top), ancestors).reshape(part, w)
    s_all = lax.all_gather(s, COL, axis=1, tiled=True)

    u = dot(f_all, strip, ((1,), (0,)))

    moved = lax.ppermute(u, ALL, [(16 * r + c, 16 * (c // 2) + 2 * r + c % 2) for r in range(8) for c in range(16)])
    u_side = lax.all_gather(moved, COL, axis=0, tiled=False).reshape(8, 2, part, w)

    u_col = jnp.zeros((NANC, 8, sub, w), jnp.float32)
    for r, t in gather_rows(u):
        u_col = lax.dynamic_update_slice(u_col, t.reshape(NANC, 1, sub, w), (0, r, 0, 0))
    s_sel = jnp.concatenate(
        [lax.dynamic_slice_in_dim(s_all, ancestors[i] * 8 * sub, 8 * sub, 1) for i in range(NANC)], axis=1
    )
    sigma = -dot(s_sel, u_col.reshape(8 * part, w), ((1,), (0,)))

    sigma_col = jnp.zeros((8, part, w), jnp.float32)
    for r, t in gather_rows(sigma):
        sigma_col = lax.dynamic_update_slice(sigma_col, t[None], (r, 0, 0))
    correction = jnp.concatenate([dot(u_side[:, p], sigma_col, ((0, 1), (0, 1))) for p in range(2)])
    sigma_child = block_inverse - correction

    blocks = sigma.reshape(NANC, sub, w)
    hit = ancestors[None, :] == lax.iota(jnp.int32, NB)[:, None]
    place = jnp.argmax(hit, axis=1)
    living = jnp.any(hit, axis=1)
    full = jnp.concatenate([lax.dynamic_slice_in_dim(blocks, place[b], 1, 0) for b in range(NB)])
    full = jnp.where(living[:, None, None], full, jnp.float32(0.0))
    back = lax.all_to_all(full.reshape(8, 3, sub, w), ROW, 0, 0, tiled=True)
    sigma_cross = back.reshape(8, 3, sub, w).transpose(1, 0, 2, 3).reshape(h, w)
    return (sigma_cross, sigma_child)


def solution(mesh):
    fine = Mesh(np.asarray(mesh.devices).reshape(4, 2, 4, 4), ALL)
    tile = P(ROW, COL)
    return jax.shard_map(
        per_device,
        mesh=fine,
        in_specs=(tile, tile, tile, tile, P()),
        out_specs=(tile, tile),
        check_vma=False,
    )
```

```python
import jax
import jax.numpy as jnp
import numpy as np
from jax import lax
from jax.experimental import pallas as pl
from jax.experimental.pallas import tpu as pltpu
from jax.sharding import Mesh, PartitionSpec as P

NB = 24
NANC = 12
ROW = ("y", "core")
COL = ("z", "x")
ALL = ("y", "core", "z", "x")
VMEM = pl.BlockSpec(memory_space=pltpu.VMEM)
SMEM = pl.BlockSpec(memory_space=pltpu.SMEM)
ANY = pl.BlockSpec(memory_space=pl.ANY)
F32 = jnp.float32


def params(mib):
    return pltpu.CompilerParams(vmem_limit_bytes=mib * 1024 * 1024)


def cost(m, k, n, in_bytes):
    return pl.CostEstimate(flops=6 * m * k * n, bytes_accessed=in_bytes, transcendentals=0)


def step(x, axis):
    if axis == "y":
        return lax.ppermute(x, ROW, [(2 * i + c, 2 * ((i + 1 - 2 * c) % 4) + c) for i in range(4) for c in range(2)])
    return lax.ppermute(x, ("core", axis), [(4 * c + i, 4 * c + (i + 1 - 2 * c) % 4) for i in range(4) for c in range(2)])


def swap(x):
    return lax.ppermute(x, "core", [(0, 1), (1, 0)])


def ring(x, axis):
    out = [x]
    for _ in range(3):
        out.append(step(out[-1], axis))
    return out


def gather_rows(x):
    mine = ring(x, "y")
    return mine + [swap(t) for t in mine]


def gather_cols(a, b):
    first = jnp.stack(ring(a, "x"))
    second = jnp.stack(ring(b, "z"))
    return ring(first, "z") + ring(second, "x")


def places():
    y, core, z, x = (lax.axis_index(n) for n in ALL)
    s = 1 - 2 * core
    back = lambda i, k: lax.rem(i - s * k + 8, 4)
    rows = [2 * back(y, k) + core for k in range(4)] + [2 * lax.rem(y + s * k + 8, 4) + 1 - core for k in range(4)]
    cols = [4 * back(z, i) + back(x, j) for i in range(4) for j in range(4)]
    cols += [4 * back(z, j) + back(x, i) for i in range(4) for j in range(4)]
    return jnp.stack(rows + cols).astype(jnp.int32)


def dot3(a, b):
    a_hi, b_hi = a.astype(jnp.bfloat16), b.astype(jnp.bfloat16)
    a_lo = (a - a_hi.astype(F32)).astype(jnp.bfloat16)
    b_lo = (b - b_hi.astype(F32)).astype(jnp.bfloat16)
    mul = lambda p, q: jnp.dot(p, q, preferred_element_type=F32)
    return mul(a_hi, b_hi) + (mul(a_hi, b_lo) + mul(a_lo, b_hi))


def col_copies(at, pieces, buf, sem, rows):
    out = []
    for i in range(32):
        half, c = i // 16, at[8 + i]
        out.append(
            pltpu.make_async_copy(
                pieces[i // 4].at[i % 4], buf.at[c, pl.ds(half * rows, rows)], sem.at[half, c]
            )
        )
    return out


def update_kernel(at, *refs):
    pieces, tiles, (u, ut), (a_buf, b_buf, a_sem, b_sem) = refs[:8], refs[8:16], refs[16:18], refs[18:]
    for i in range(8):
        pltpu.make_async_copy(tiles[i], b_buf.at[at[i]], b_sem.at[at[i]]).start()
    for copy in col_copies(at, pieces, a_buf, a_sem, a_buf.shape[1] // 2):
        copy.start()
    u[...] = jnp.zeros_like(u)
    rows = a_buf.shape[1] // 2

    def body(j, carry):
        pltpu.make_async_copy(tiles[0], b_buf.at[j], b_sem.at[j]).wait()
        for k in range(2):
            for half in range(2):
                pltpu.make_async_copy(
                    pieces[0].at[0], a_buf.at[2 * j + k, pl.ds(half * rows, rows)], a_sem.at[half, 2 * j + k]
                ).wait()
        lhs = jnp.concatenate([a_buf[2 * j], a_buf[2 * j + 1]], axis=1)
        u[...] += dot3(lhs, b_buf[j])
        return carry

    lax.fori_loop(0, 8, body, 0)
    ut[...] = u[...].T


def update_product(at, pieces, tiles):
    m, w = 2 * pieces[0].shape[1], pieces[0].shape[2]
    h = tiles[0].shape[0]
    out = jax.ShapeDtypeStruct((m, w), F32)
    return pl.pallas_call(
        update_kernel,
        out_shape=(out, jax.ShapeDtypeStruct((w, m), F32)),
        in_specs=[SMEM] + [ANY] * 16,
        out_specs=(VMEM, VMEM),
        scratch_shapes=[
            pltpu.VMEM((16, m, w), F32),
            pltpu.VMEM((8, h, w), F32),
            pltpu.SemaphoreType.DMA((2, 16)),
            pltpu.SemaphoreType.DMA((8,)),
        ],
        compiler_params=params(40),
        cost_estimate=cost(m, 8 * h, w, 4 * 16 * w * (m + w)),
        name="update",
    )(at, *pieces, *tiles)


def cross_kernel(at, *refs):
    pieces, tiles, (sigma,), (s_buf, u_buf, s_sem, u_sem) = refs[:8], refs[8:16], refs[16:17], refs[17:]
    width = s_buf.shape[2] // 2
    copies = []
    for i in range(32):
        half, c = i // 16, at[8 + i]
        copies.append(
            pltpu.make_async_copy(
                pieces[i // 4].at[i % 4], s_buf.at[c, :, pl.ds(half * width, width)], s_sem.at[half, c]
            )
        )
    for i in range(8):
        copies.append(pltpu.make_async_copy(tiles[i], u_buf.at[:, at[i]], u_sem.at[at[i]]))
    for copy in copies:
        copy.start()
    sigma[...] = jnp.zeros_like(sigma)
    for copy in copies:
        copy.wait()
    m, w = sigma.shape

    def body(k, carry):
        lhs = s_buf[:, :, pl.ds(pl.multiple_of(k * 768, 128), 768)].reshape(m, 768)
        rhs = u_buf[pl.ds(3 * k, 3)].reshape(768, w)
        sigma[...] -= dot3(lhs, rhs)
        return carry

    lax.fori_loop(0, 4, body, 0)


def cross_product(at, pieces, tiles):
    q, half = pieces[0].shape[1:]
    sub, w = tiles[0].shape[1:]
    return pl.pallas_call(
        cross_kernel,
        out_shape=jax.ShapeDtypeStruct((16 * q, w), F32),
        in_specs=[SMEM] + [ANY] * 16,
        out_specs=VMEM,
        scratch_shapes=[
            pltpu.VMEM((16, q, 2 * half), F32),
            pltpu.VMEM((NANC, 8, sub, w), F32),
            pltpu.SemaphoreType.DMA((2, 16)),
            pltpu.SemaphoreType.DMA((8,)),
        ],
        compiler_params=params(40),
        cost_estimate=cost(16 * q, 2 * half, w, 4 * 2 * half * (16 * q + w)),
        name="cross",
    )(at, *pieces, *tiles)


def child_kernel(at, base, *refs):
    pieces, tiles, (child,), (a_buf, b_buf, a_sem, b_sem) = refs[:8], refs[8:16], refs[16:17], refs[17:]
    w = a_buf.shape[2]
    copies = col_copies(at, pieces, a_buf, a_sem, w // 2)
    for i in range(8):
        copies.append(pltpu.make_async_copy(tiles[i], b_buf.at[at[i]], b_sem.at[at[i]]))
    for copy in copies:
        copy.start()
    child[...] = base[...]
    for copy in copies:
        copy.wait()

    def body(j, carry):
        rhs = b_buf[pl.ds(2 * j, 2)].reshape(2 * w, w)
        for p in range(2):
            lhs = jnp.concatenate([a_buf[4 * j + p], a_buf[4 * j + 2 + p]], axis=1)
            child[pl.ds(p * w, w)] -= dot3(lhs, rhs)
        return carry

    lax.fori_loop(0, 4, body, 0)


def child_product(at, base, pieces, tiles):
    h, w = base.shape
    return pl.pallas_call(
        child_kernel,
        out_shape=jax.ShapeDtypeStruct((h, w), F32),
        in_specs=[SMEM, VMEM] + [ANY] * 16,
        out_specs=VMEM,
        scratch_shapes=[
            pltpu.VMEM((16, w, w), F32),
            pltpu.VMEM((8, w, w), F32),
            pltpu.SemaphoreType.DMA((2, 16)),
            pltpu.SemaphoreType.DMA((8,)),
        ],
        compiler_params=params(40),
        cost_estimate=cost(h, 8 * w, w, 4 * w * 8 * (h + w)),
        name="child",
    )(at, base, *pieces, *tiles)


def spread(x):
    h, w = x.shape
    sub = h // 24
    return lax.all_to_all(x.reshape(3, 8, sub, w), ROW, 1, 0, tiled=True).reshape(NB, sub, w)


def pick_rows_kernel(anc, x, a, b):
    for i in range(NANC // 2):
        a[i] = x[anc[i]]
        b[i] = x[anc[i + NANC // 2]]


def pick_rows(ancestors, x):
    sub, w = x.shape[1:]
    out = jax.ShapeDtypeStruct((NANC // 2, sub, w), F32)
    a, b = pl.pallas_call(
        pick_rows_kernel,
        out_shape=(out, out),
        in_specs=[SMEM, VMEM],
        out_specs=(VMEM, VMEM),
        compiler_params=params(8),
        name="pick_rows",
    )(ancestors, x)
    return a.reshape(-1, w), b.reshape(-1, w)


def pick_cols_kernel(anc, x, a, b):
    for out, first in ((a, 0), (b, NANC // 2)):
        for i in range(NANC // 2):
            for k in range(2):
                t = 2 * anc[first + i] + k
                off = pl.multiple_of(lax.rem(t, 3) * 128, 128)
                out[:, pl.ds(i * 256 + k * 128, 128)] = x[lax.div(t, 3), :, pl.ds(off, 128)]


def pick_cols(ancestors, x):
    q = x.shape[1]
    out = jax.ShapeDtypeStruct((q, NANC * 128), F32)
    return pl.pallas_call(
        pick_cols_kernel,
        out_shape=(out, out),
        in_specs=[SMEM, VMEM],
        out_specs=(VMEM, VMEM),
        compiler_params=params(8),
        name="pick_cols",
    )(ancestors, x)


def place_kernel(anc, x, out):
    out[...] = jnp.zeros_like(out)
    for i in range(NANC):
        out[anc[i]] = x[i]


def place_rows(ancestors, x):
    sub, w = x.shape[1:]
    return pl.pallas_call(
        place_kernel,
        out_shape=jax.ShapeDtypeStruct((NB, sub, w), F32),
        in_specs=[SMEM, VMEM],
        out_specs=VMEM,
        compiler_params=params(8),
        name="place_rows",
    )(ancestors, x)


def per_device(sigma_top, factor_cross, factor_inverse, block_inverse, ancestors):
    h, w = sigma_top.shape
    sub = h // 24
    at = places()

    f_pieces = gather_cols(*pick_rows(ancestors, spread(factor_cross)))
    inverse_tiles = gather_rows(factor_inverse)

    s_rows = jnp.concatenate(pick_rows(ancestors, spread(sigma_top)))
    s_cols = lax.all_to_all(s_rows.reshape(16, -1, w), COL, 0, 0, tiled=True)
    s_pieces = gather_cols(*pick_cols(ancestors, s_cols))

    u, ut = update_product(at, f_pieces, inverse_tiles)
    moved = lax.ppermute(ut, ALL, [(16 * r + c, 16 * (c // 2) + 2 * r + c % 2) for r in range(8) for c in range(16)])
    u_pieces = gather_cols(moved[: w // 2], moved[w // 2 :])
    u_tiles = gather_rows(u.reshape(NANC, sub, w))

    sigma = cross_product(at, s_pieces, u_tiles)
    sigma_tiles = gather_rows(sigma)
    sigma_child = child_product(at, block_inverse, u_pieces, sigma_tiles)

    full = place_rows(ancestors, sigma.reshape(NANC, sub, w))
    back = lax.all_to_all(full.reshape(8, 3, sub, w), ROW, 0, 0, tiled=True)
    sigma_cross = back.reshape(8, 3, sub, w).transpose(1, 0, 2, 3).reshape(h, w)
    return (sigma_cross, sigma_child)


def solution(mesh):
    fine = Mesh(np.asarray(mesh.devices).reshape(4, 2, 4, 4), ALL)
    tile = P(ROW, COL)
    return jax.shard_map(
        per_device,
        mesh=fine,
        in_specs=(tile, tile, tile, tile, P()),
        out_specs=(tile, tile),
        check_vma=False,
    )
```

```python
import jax
import jax.numpy as jnp
import numpy as np
from jax import lax
from jax.experimental import pallas as pl
from jax.experimental.pallas import tpu as pltpu
from jax.sharding import Mesh, PartitionSpec as P

NB = 24
NANC = 12
ROW = ("y", "core")
COL = ("z", "x")
ALL = ("y", "core", "z", "x")
VMEM = pl.BlockSpec(memory_space=pltpu.VMEM)
SMEM = pl.BlockSpec(memory_space=pltpu.SMEM)
ANY = pl.BlockSpec(memory_space=pl.ANY)
F32 = jnp.float32


def params(mib):
    return pltpu.CompilerParams(vmem_limit_bytes=mib * 1024 * 1024)


def cost(m, k, n, in_bytes):
    return pl.CostEstimate(flops=6 * m * k * n, bytes_accessed=in_bytes, transcendentals=0)


def step(x, axis):
    if axis == "y":
        return lax.ppermute(x, ROW, [(2 * i + c, 2 * ((i + 1 - 2 * c) % 4) + c) for i in range(4) for c in range(2)])
    return lax.ppermute(x, ("core", axis), [(4 * c + i, 4 * c + (i + 1 - 2 * c) % 4) for i in range(4) for c in range(2)])


def swap(x):
    return lax.ppermute(x, "core", [(0, 1), (1, 0)])


def after(x, *others):
    return lax.optimization_barrier((x, *others))[0]


def ring(x, axis, gates=((), (), ())):
    out = [x]
    for gate in gates:
        out.append(step(after(out[-1], *gate) if gate else out[-1], axis))
    return out


def gather_rows(x, gates=((), (), ())):
    mine = ring(x, "y", gates)
    return mine + [swap(t) for t in mine]


def first_axis(a, b, gates=((), (), ())):
    return jnp.stack(ring(a, "x", gates)), jnp.stack(ring(b, "z", gates))


def second_axis(first, second, gates=((), (), ())):
    return ring(first, "z", gates) + ring(second, "x", gates)


def gather_cols(a, b, gates=((), (), ())):
    return second_axis(*first_axis(a, b, gates))


def deal_cols(x, gate):
    x = x.reshape(4, 4, -1, x.shape[1])
    at = lax.axis_index("x")
    out = [lax.dynamic_index_in_dim(x, at, 1, False)]
    for k in range(1, 4):
        part = lax.dynamic_index_in_dim(x, lax.rem(at + k, 4), 1, False)
        out.append(lax.ppermute(part, "x", [(i, (i + k) % 4) for i in range(4)]))
    x = after(jnp.stack(out, axis=1), *gate)
    at = lax.axis_index("z")
    out = [lax.dynamic_index_in_dim(x, at, 0, False)]
    for k in range(1, 4):
        part = lax.dynamic_index_in_dim(x, lax.rem(at + k, 4), 0, False)
        out.append(lax.ppermute(part, "z", [(i, (i + k) % 4) for i in range(4)]))
    return jnp.stack(out)


def places():
    y, core, z, x = (lax.axis_index(n) for n in ALL)
    s = 1 - 2 * core
    back = lambda i, k: lax.rem(i - s * k + 8, 4)
    rows = [2 * back(y, k) + core for k in range(4)] + [2 * lax.rem(y + s * k + 8, 4) + 1 - core for k in range(4)]
    cols = [4 * back(z, i) + back(x, j) for i in range(4) for j in range(4)]
    cols += [4 * back(z, j) + back(x, i) for i in range(4) for j in range(4)]
    return jnp.stack(rows + cols).astype(jnp.int32)


def dot3(a, b):
    a_hi, b_hi = a.astype(jnp.bfloat16), b.astype(jnp.bfloat16)
    a_lo = (a - a_hi.astype(F32)).astype(jnp.bfloat16)
    b_lo = (b - b_hi.astype(F32)).astype(jnp.bfloat16)
    mul = lambda p, q: jnp.dot(p, q, preferred_element_type=F32)
    return mul(a_hi, b_hi) + (mul(a_hi, b_lo) + mul(a_lo, b_hi))


def col_copies(at, pieces, buf, sem, rows):
    out = []
    for i in range(32):
        half, c = i // 16, at[8 + i]
        out.append(
            pltpu.make_async_copy(
                pieces[i // 4].at[i % 4], buf.at[c, pl.ds(half * rows, rows)], sem.at[half, c]
            )
        )
    return out


def update_kernel(at, *refs):
    pieces, tiles, (u, ut), (a_buf, b_buf, a_sem, b_sem) = refs[:8], refs[8:16], refs[16:18], refs[18:]
    for i in range(8):
        pltpu.make_async_copy(tiles[i], b_buf.at[at[i]], b_sem.at[at[i]]).start()
    for copy in col_copies(at, pieces, a_buf, a_sem, a_buf.shape[1] // 2):
        copy.start()
    u[...] = jnp.zeros_like(u)
    rows = a_buf.shape[1] // 2

    def body(j, carry):
        pltpu.make_async_copy(tiles[0], b_buf.at[j], b_sem.at[j]).wait()
        for k in range(2):
            for half in range(2):
                pltpu.make_async_copy(
                    pieces[0].at[0], a_buf.at[2 * j + k, pl.ds(half * rows, rows)], a_sem.at[half, 2 * j + k]
                ).wait()
        lhs = jnp.concatenate([a_buf[2 * j], a_buf[2 * j + 1]], axis=1)
        u[...] += dot3(lhs, b_buf[j])
        return carry

    lax.fori_loop(0, 8, body, 0)
    ut[...] = u[...].T


def update_product(at, pieces, tiles):
    m, w = 2 * pieces[0].shape[1], pieces[0].shape[2]
    h = tiles[0].shape[0]
    out = jax.ShapeDtypeStruct((m, w), F32)
    return pl.pallas_call(
        update_kernel,
        out_shape=(out, jax.ShapeDtypeStruct((w, m), F32)),
        in_specs=[SMEM] + [ANY] * 16,
        out_specs=(VMEM, VMEM),
        scratch_shapes=[
            pltpu.VMEM((16, m, w), F32),
            pltpu.VMEM((8, h, w), F32),
            pltpu.SemaphoreType.DMA((2, 16)),
            pltpu.SemaphoreType.DMA((8,)),
        ],
        compiler_params=params(40),
        cost_estimate=cost(m, 8 * h, w, 4 * 16 * w * (m + w)),
        name="update",
    )(at, *pieces, *tiles)


def cross_kernel(at, *refs):
    pieces, tiles, (sigma,), (s_buf, u_buf, s_sem, u_sem) = refs[:8], refs[8:16], refs[16:17], refs[17:]
    width = s_buf.shape[2] // 2
    copies = []
    for i in range(32):
        half, c = i // 16, at[8 + i]
        copies.append(
            pltpu.make_async_copy(
                pieces[i // 4].at[i % 4], s_buf.at[c, :, pl.ds(half * width, width)], s_sem.at[half, c]
            )
        )
    for i in range(8):
        copies.append(pltpu.make_async_copy(tiles[i], u_buf.at[:, at[i]], u_sem.at[at[i]]))
    for copy in copies:
        copy.start()
    sigma[...] = jnp.zeros_like(sigma)
    for copy in copies:
        copy.wait()
    m, w = sigma.shape

    def body(k, carry):
        lhs = s_buf[:, :, pl.ds(pl.multiple_of(k * 768, 128), 768)].reshape(m, 768)
        rhs = u_buf[pl.ds(3 * k, 3)].reshape(768, w)
        sigma[...] -= dot3(lhs, rhs)
        return carry

    lax.fori_loop(0, 4, body, 0)


def cross_product(at, pieces, tiles):
    q, half = pieces[0].shape[1:]
    sub, w = tiles[0].shape[1:]
    return pl.pallas_call(
        cross_kernel,
        out_shape=jax.ShapeDtypeStruct((16 * q, w), F32),
        in_specs=[SMEM] + [ANY] * 16,
        out_specs=VMEM,
        scratch_shapes=[
            pltpu.VMEM((16, q, 2 * half), F32),
            pltpu.VMEM((NANC, 8, sub, w), F32),
            pltpu.SemaphoreType.DMA((2, 16)),
            pltpu.SemaphoreType.DMA((8,)),
        ],
        compiler_params=params(40),
        cost_estimate=cost(16 * q, 2 * half, w, 4 * 2 * half * (16 * q + w)),
        name="cross",
    )(at, *pieces, *tiles)


def child_kernel(at, base, *refs):
    pieces, tiles, (child,), (a_buf, b_buf, a_sem, b_sem) = refs[:8], refs[8:16], refs[16:17], refs[17:]
    w = a_buf.shape[2]
    copies = col_copies(at, pieces, a_buf, a_sem, w // 2)
    for i in range(8):
        copies.append(pltpu.make_async_copy(tiles[i], b_buf.at[at[i]], b_sem.at[at[i]]))
    for copy in copies:
        copy.start()
    child[...] = base[...]
    for copy in copies:
        copy.wait()

    def body(j, carry):
        rhs = b_buf[pl.ds(2 * j, 2)].reshape(2 * w, w)
        for p in range(2):
            lhs = jnp.concatenate([a_buf[4 * j + p], a_buf[4 * j + 2 + p]], axis=1)
            child[pl.ds(p * w, w)] -= dot3(lhs, rhs)
        return carry

    lax.fori_loop(0, 4, body, 0)


def child_product(at, base, pieces, tiles):
    h, w = base.shape
    return pl.pallas_call(
        child_kernel,
        out_shape=jax.ShapeDtypeStruct((h, w), F32),
        in_specs=[SMEM, VMEM] + [ANY] * 16,
        out_specs=VMEM,
        scratch_shapes=[
            pltpu.VMEM((16, w, w), F32),
            pltpu.VMEM((8, w, w), F32),
            pltpu.SemaphoreType.DMA((2, 16)),
            pltpu.SemaphoreType.DMA((8,)),
        ],
        compiler_params=params(40),
        cost_estimate=cost(h, 8 * w, w, 4 * w * 8 * (h + w)),
        name="child",
    )(at, base, *pieces, *tiles)


def spread(x):
    h, w = x.shape
    sub = h // 24
    return lax.all_to_all(x.reshape(3, 8, sub, w), ROW, 1, 0, tiled=True).reshape(NB, sub, w)


def pick_rows_kernel(anc, x, a, b):
    for i in range(NANC // 2):
        a[i] = x[anc[i]]
        b[i] = x[anc[i + NANC // 2]]


def pick_rows(ancestors, x):
    sub, w = x.shape[1:]
    out = jax.ShapeDtypeStruct((NANC // 2, sub, w), F32)
    a, b = pl.pallas_call(
        pick_rows_kernel,
        out_shape=(out, out),
        in_specs=[SMEM, VMEM],
        out_specs=(VMEM, VMEM),
        compiler_params=params(8),
        name="pick_rows",
    )(ancestors, x)
    return a.reshape(-1, w), b.reshape(-1, w)


def pick_cols_kernel(anc, at, x, a, b):
    for out, first in ((a, 0), (b, NANC // 2)):
        for i in range(NANC // 2):
            for k in range(2):
                t = 2 * anc[first + i] + k
                off = pl.multiple_of(lax.rem(t, 3) * 128, 128)
                c = lax.div(t, 3)
                back_z = lax.rem(at[0] - lax.div(c, 4) + 4, 4)
                back_x = lax.rem(at[1] - lax.rem(c, 4) + 4, 4)
                out[:, pl.ds(i * 256 + k * 128, 128)] = x[back_z, back_x, :, pl.ds(off, 128)]


def pick_cols(ancestors, x):
    q = x.shape[2]
    at = jnp.stack([lax.axis_index(n) for n in COL]).astype(jnp.int32)
    out = jax.ShapeDtypeStruct((q, NANC * 128), F32)
    return pl.pallas_call(
        pick_cols_kernel,
        out_shape=(out, out),
        in_specs=[SMEM, SMEM, VMEM],
        out_specs=(VMEM, VMEM),
        compiler_params=params(8),
        name="pick_cols",
    )(ancestors, at, x)


def place_kernel(anc, x, out):
    out[...] = jnp.zeros_like(out)
    for i in range(NANC):
        out[anc[i]] = x[i]


def place_rows(ancestors, x):
    sub, w = x.shape[1:]
    return pl.pallas_call(
        place_kernel,
        out_shape=jax.ShapeDtypeStruct((NB, sub, w), F32),
        in_specs=[SMEM, VMEM],
        out_specs=VMEM,
        compiler_params=params(8),
        name="place_rows",
    )(ancestors, x)


def per_device(sigma_top, factor_cross, factor_inverse, block_inverse, ancestors):
    h, w = sigma_top.shape
    sub = h // 24
    at = places()

    f_once = first_axis(*pick_rows(ancestors, spread(factor_cross)))
    f_pieces = second_axis(*f_once)
    inverse_tiles = gather_rows(factor_inverse, ((), (), (f_pieces[1], f_pieces[5])))

    s_rows = jnp.concatenate(pick_rows(ancestors, spread(after(sigma_top, *f_once))))
    s_cols = deal_cols(after(s_rows, f_pieces[1], f_pieces[5]), (f_pieces[2], f_pieces[6]))
    s_once = first_axis(*pick_cols(ancestors, s_cols))

    u, ut = update_product(at, f_pieces, inverse_tiles)
    moved = lax.ppermute(ut, ALL, [(16 * r + c, 16 * (c // 2) + 2 * r + c % 2) for r in range(8) for c in range(16)])
    s_pieces = second_axis(*s_once)
    u_pieces = gather_cols(moved[: w // 2], moved[w // 2 :])
    u_tiles = gather_rows(u.reshape(NANC, sub, w))

    sigma = cross_product(at, s_pieces, u_tiles)
    sigma_tiles = gather_rows(sigma)
    sigma_child = child_product(at, block_inverse, u_pieces, sigma_tiles)

    full = place_rows(ancestors, sigma.reshape(NANC, sub, w))
    back = lax.all_to_all(full.reshape(8, 3, sub, w), ROW, 0, 0, tiled=True)
    sigma_cross = back.reshape(8, 3, sub, w).transpose(1, 0, 2, 3).reshape(h, w)
    return (sigma_cross, sigma_child)


def solution(mesh):
    fine = Mesh(np.asarray(mesh.devices).reshape(4, 2, 4, 4), ALL)
    tile = P(ROW, COL)
    return jax.shard_map(
        per_device,
        mesh=fine,
        in_specs=(tile, tile, tile, tile, P()),
        out_specs=(tile, tile),
        check_vma=False,
    )
```

```python
import functools

import jax
import jax.numpy as jnp
import numpy as np
from jax import lax
from jax.experimental import pallas as pl
from jax.experimental.pallas import tpu as pltpu
from jax.sharding import Mesh, PartitionSpec as P

NB = 24
NANC = 12
ROW = ("y", "core")
COL = ("z", "x")
ALL = ("y", "core", "z", "x")
VMEM = pl.BlockSpec(memory_space=pltpu.VMEM)
SMEM = pl.BlockSpec(memory_space=pltpu.SMEM)
ANY = pl.BlockSpec(memory_space=pl.ANY)
F32 = jnp.float32


def params(mib):
    return pltpu.CompilerParams(vmem_limit_bytes=mib * 1024 * 1024)


def cost(m, k, n, in_bytes):
    return pl.CostEstimate(flops=6 * m * k * n, bytes_accessed=in_bytes, transcendentals=0)


def after(x, *others):
    return lax.optimization_barrier((x, *others))[0]


def step(x):
    return lax.ppermute(x, ROW, [(2 * i + c, 2 * ((i + 1 - 2 * c) % 4) + c) for i in range(4) for c in range(2)])


def swap(x):
    return lax.ppermute(x, "core", [(0, 1), (1, 0)])


def gather_rows(x):
    mine = [x]
    for _ in range(3):
        mine.append(step(mine[-1]))
    return mine + [swap(t) for t in mine]


def hop(x, along, by):
    pairs = []
    for core in range(2):
        for i in range(4):
            for j in range(4):
                to = (i, (j + by) % 4) if along == core else ((i + by) % 4, j)
                pairs.append((16 * core + 4 * i + j, 16 * core + 4 * to[0] + to[1]))
    return lax.ppermute(x, ("core",) + COL, pairs)


def gather_cols(x, axis, gates=((), (), ())):
    half = x.shape[axis] // 2
    up, down = hop(x, 0, 1), hop(x, 0, -1)
    top = hop(lax.slice_in_dim(after(up, *gates[0]), 0, half, axis=axis), 0, 1)
    low = hop(lax.slice_in_dim(after(down, *gates[0]), half, 2 * half, axis=axis), 0, -1)
    group = after(jnp.stack([x, up, down, jnp.concatenate([top, low], axis=axis)]), *gates[1])
    up, down = hop(group, 1, 1), hop(group, 1, -1)
    return (group, up, down), (hop(after(up, *gates[2])[:2], 1, 1), hop(after(down, *gates[2])[2:], 1, -1))


def places():
    y, core, z, x = (lax.axis_index(n) for n in ALL)
    s = 1 - 2 * core
    near = lambda i, k: lax.rem(i + k + 8, 4)
    rows = [2 * near(y, -s * k) + core for k in range(4)] + [2 * near(y, s * k) + 1 - core for k in range(4)]
    first, second = jnp.where(core == 0, x, z), jnp.where(core == 0, z, x)
    cols = []
    for k in (0, -1, 1, 2):
        for i in (0, -1, 1, 2):
            u, v = near(first, i), near(second, k)
            cols.append(jnp.where(core == 0, 4 * v + u, 4 * u + v))
    return jnp.stack(rows + cols).astype(jnp.int32)


def dot3(a, b):
    a_hi, b_hi = a.astype(jnp.bfloat16), b.astype(jnp.bfloat16)
    a_lo = (a - a_hi.astype(F32)).astype(jnp.bfloat16)
    b_lo = (b - b_hi.astype(F32)).astype(jnp.bfloat16)
    mul = lambda p, q: jnp.dot(p, q, preferred_element_type=F32)
    return mul(a_hi, b_hi) + (mul(a_hi, b_lo) + mul(a_lo, b_hi))


def pair_dot(at, tile, a_buf, slot, b_buf, per):
    def one(k):
        return a_buf[slot + k], b_buf[lax.div(at[tile + k], per)]

    def body(q):
        (a0, b0), (a1, b1) = one(q), one(3 - q)
        return dot3(jnp.concatenate([a0, a1], axis=1), jnp.concatenate([b0, b1], axis=0))

    return body


def near_kernel(per, at, *refs):
    groups, tiles, (acc, far), (a_buf, b_buf, a_sem, b_sem) = refs[:3], refs[3:11], refs[11:13], refs[13:]
    outs = acc.shape[0]
    many = tiles[0].shape[0]
    copies = [
        pltpu.make_async_copy(tiles[i], b_buf.at[pl.ds(at[i] * many, many)], b_sem.at[i]) for i in range(8)
    ]
    copies += [pltpu.make_async_copy(groups[i], a_buf.at[pl.ds(4 * i, 4)], a_sem.at[i]) for i in range(3)]
    for copy in copies:
        copy.start()
    acc[...] = jnp.zeros_like(acc)
    for copy in copies:
        copy.wait()
    for k in range(4):
        far[k] = b_buf[lax.div(at[20 + k], per)]

    def body(i, carry):
        g, q = lax.div(i, 2), lax.rem(i, 2)
        p = lax.rem(at[8 + 4 * g + q], outs)
        acc[p] += pair_dot(at, 8 + 4 * g, a_buf, 4 * g, b_buf, per)(q)
        return carry

    lax.fori_loop(0, 6, body, 0)


def near_product(at, groups, tiles, outs):
    m, w = groups[0].shape[1:]
    many, k, n = tiles[0].shape
    return pl.pallas_call(
        functools.partial(near_kernel, 16 // (8 * many)),
        out_shape=(jax.ShapeDtypeStruct((outs, m, n), F32), jax.ShapeDtypeStruct((4, k, n), F32)),
        in_specs=[SMEM] + [ANY] * 11,
        out_specs=(VMEM, VMEM),
        scratch_shapes=[
            pltpu.VMEM((12, m, w), F32),
            pltpu.VMEM((8 * many, k, n), F32),
            pltpu.SemaphoreType.DMA((3,)),
            pltpu.SemaphoreType.DMA((8,)),
        ],
        compiler_params=params(40),
        cost_estimate=cost(m, 12 * w, n, 4 * w * (12 * m + 8 * many * n)),
        name="near",
    )(at, *groups, *tiles)


def far_sum(at, acc, top, low, far, a_buf, sem):
    copies = [pltpu.make_async_copy(top, a_buf.at[pl.ds(0, 2)], sem.at[0])]
    copies += [pltpu.make_async_copy(low, a_buf.at[pl.ds(2, 2)], sem.at[1])]
    for copy in copies:
        copy.start()
    for copy in copies:
        copy.wait()
    for q in range(2):
        yield q, dot3(
            jnp.concatenate([a_buf[q], a_buf[3 - q]], axis=1), jnp.concatenate([far[q], far[3 - q]], axis=0)
        )


def update_kernel(at, acc, top, low, far, u, ut, a_buf, sem):
    total = acc[0]
    for _, part in far_sum(at, acc, top, low, far, a_buf, sem):
        total += part
    u[...] = total
    ut[...] = total.T


def update_product(at, acc, top, low, far):
    _, m, n = acc.shape
    return pl.pallas_call(
        update_kernel,
        out_shape=(jax.ShapeDtypeStruct((m, n), F32), jax.ShapeDtypeStruct((n, m), F32)),
        in_specs=[SMEM, VMEM, ANY, ANY, VMEM],
        out_specs=(VMEM, VMEM),
        scratch_shapes=[pltpu.VMEM((4,) + top.shape[1:], F32), pltpu.SemaphoreType.DMA((2,))],
        compiler_params=params(24),
        cost_estimate=cost(m, 4 * top.shape[2], n, 16 * m * n),
        name="update",
    )(at, acc, top, low, far)


def child_kernel(at, acc, top, low, far, base, child, a_buf, sem):
    w = acc.shape[1]
    for p in range(2):
        child[pl.ds(p * w, w)] = base[pl.ds(p * w, w)] - acc[p]
    for q, part in far_sum(at, acc, top, low, far, a_buf, sem):
        p = pl.multiple_of(lax.rem(at[20 + q], 2) * w, 8)
        child[pl.ds(p, w)] -= part


def child_product(at, acc, top, low, far, base):
    return pl.pallas_call(
        child_kernel,
        out_shape=jax.ShapeDtypeStruct(base.shape, F32),
        in_specs=[SMEM, VMEM, ANY, ANY, VMEM, VMEM],
        out_specs=VMEM,
        scratch_shapes=[pltpu.VMEM((4,) + top.shape[1:], F32), pltpu.SemaphoreType.DMA((2,))],
        compiler_params=params(24),
        cost_estimate=cost(acc.shape[1], 4 * top.shape[2], acc.shape[2], 24 * acc.shape[1] * acc.shape[2]),
        name="child",
    )(at, acc, top, low, far, base)


def cross_kernel(at, *refs):
    groups, (top, low), tiles, (sigma,), (s_buf, u_buf, s_sem, u_sem) = (
        refs[:3], refs[3:5], refs[5:13], refs[13:14], refs[14:]
    )
    pieces = [g.at[i] for g in groups for i in range(4)] + [g.at[i] for g in (top, low) for i in range(2)]
    copies = [pltpu.make_async_copy(pieces[i], s_buf.at[at[8 + i]], s_sem.at[i]) for i in range(16)]
    copies += [pltpu.make_async_copy(tiles[i], u_buf.at[:, at[i]], u_sem.at[i]) for i in range(8)]
    for copy in copies:
        copy.start()
    sigma[...] = jnp.zeros_like(sigma)
    for copy in copies:
        copy.wait()
    m, w = sigma.shape

    def body(k, carry):
        lhs = s_buf[:, :, pl.ds(pl.multiple_of(k * 768, 128), 768)].reshape(m, 768)
        rhs = u_buf[pl.ds(3 * k, 3)].reshape(768, w)
        sigma[...] -= dot3(lhs, rhs)
        return carry

    lax.fori_loop(0, 4, body, 0)


def cross_product(at, near, far, tiles):
    q, width = near[0].shape[1:]
    sub, w = tiles[0].shape[1:]
    return pl.pallas_call(
        cross_kernel,
        out_shape=jax.ShapeDtypeStruct((16 * q, w), F32),
        in_specs=[SMEM] + [ANY] * 13,
        out_specs=VMEM,
        scratch_shapes=[
            pltpu.VMEM((16, q, width), F32),
            pltpu.VMEM((NANC, 8, sub, w), F32),
            pltpu.SemaphoreType.DMA((16,)),
            pltpu.SemaphoreType.DMA((8,)),
        ],
        compiler_params=params(40),
        cost_estimate=cost(16 * q, width, w, 4 * width * (16 * q + w)),
        name="cross",
    )(at, *near, *far, *tiles)


def spread(x):
    h, w = x.shape
    sub = h // 24
    return lax.all_to_all(x.reshape(3, 8, sub, w), ROW, 1, 0, tiled=True).reshape(NB, sub, w)


def pick_rows_kernel(anc, x, out):
    for i in range(NANC):
        out[i] = x[anc[i]]


def pick_rows(ancestors, x):
    sub, w = x.shape[1:]
    return pl.pallas_call(
        pick_rows_kernel,
        out_shape=jax.ShapeDtypeStruct((NANC, sub, w), F32),
        in_specs=[SMEM, VMEM],
        out_specs=VMEM,
        compiler_params=params(8),
        name="pick_rows",
    )(ancestors, x).reshape(NANC * sub, w)


def pick_cols_kernel(anc, x, out):
    for i in range(NANC):
        for k in range(2):
            t = 2 * anc[i] + k
            off = pl.multiple_of(lax.rem(t, 3) * 128, 128)
            out[:, pl.ds(i * 256 + k * 128, 128)] = x[lax.div(t, 3), :, pl.ds(off, 128)]


def pick_cols(ancestors, x):
    return pl.pallas_call(
        pick_cols_kernel,
        out_shape=jax.ShapeDtypeStruct((x.shape[1], NANC * 256), F32),
        in_specs=[SMEM, VMEM],
        out_specs=VMEM,
        compiler_params=params(8),
        name="pick_cols",
    )(ancestors, x)


def place_kernel(anc, x, out):
    out[...] = jnp.zeros_like(out)
    for i in range(NANC):
        out[anc[i]] = x[i]


def place_rows(ancestors, x):
    sub, w = x.shape[1:]
    return pl.pallas_call(
        place_kernel,
        out_shape=jax.ShapeDtypeStruct((NB, sub, w), F32),
        in_specs=[SMEM, VMEM],
        out_specs=VMEM,
        compiler_params=params(8),
        name="place_rows",
    )(ancestors, x)


def per_device(sigma_top, factor_cross, factor_inverse, block_inverse, ancestors):
    h, w = sigma_top.shape
    sub = h // 24
    at = places()

    f = pick_rows(ancestors, spread(factor_cross))
    inverse_tiles = [t.reshape(2, w, w) for t in gather_rows(factor_inverse)]
    f_near, f_far = gather_cols(f, 0)

    s = pick_rows(ancestors, spread(after(sigma_top, f)))
    s_cols = lax.all_to_all(after(s, f_near[0]).reshape(16, -1, w), COL, 0, 0, tiled=True)
    s_near, s_far = gather_cols(after(pick_cols(ancestors, s_cols), f_near[1], f_near[2]), 1, (f_far, (), ()))

    acc, b_far = near_product(at, f_near, inverse_tiles, 1)
    u, ut = update_product(at, acc, *f_far, b_far)

    moved = lax.ppermute(ut, ALL, [(16 * r + c, 16 * (c // 2) + 2 * r + c % 2) for r in range(8) for c in range(16)])
    u_near, u_far = gather_cols(moved, 0)
    u_tiles = gather_rows(u.reshape(NANC, sub, w))

    sigma = cross_product(at, s_near, s_far, u_tiles)
    sigma_tiles = [t[None] for t in gather_rows(sigma)]
    acc, b_far = near_product(at, u_near, sigma_tiles, 2)
    sigma_child = child_product(at, acc, *u_far, b_far, block_inverse)

    full = place_rows(ancestors, sigma.reshape(NANC, sub, w))
    back = lax.all_to_all(full.reshape(8, 3, sub, w), ROW, 0, 0, tiled=True)
    sigma_cross = back.reshape(8, 3, sub, w).transpose(1, 0, 2, 3).reshape(h, w)
    return (sigma_cross, sigma_child)


def solution(mesh):
    fine = Mesh(np.asarray(mesh.devices).reshape(4, 2, 4, 4), ALL)
    tile = P(ROW, COL)
    return jax.shard_map(
        per_device,
        mesh=fine,
        in_specs=(tile, tile, tile, tile, P()),
        out_specs=(tile, tile),
        check_vma=False,
    )
```

```python
import functools

import jax
import jax.numpy as jnp
import numpy as np
from jax import lax
from jax.experimental import pallas as pl
from jax.experimental.pallas import tpu as pltpu
from jax.sharding import Mesh, PartitionSpec as P

NB = 24
NANC = 12
ROW = ("y", "core")
COL = ("z", "x")
ALL = ("y", "core", "z", "x")
VMEM = pl.BlockSpec(memory_space=pltpu.VMEM)
SMEM = pl.BlockSpec(memory_space=pltpu.SMEM)
ANY = pl.BlockSpec(memory_space=pl.ANY)
F32 = jnp.float32


def params(mib):
    return pltpu.CompilerParams(vmem_limit_bytes=mib * 1024 * 1024)


def cost(m, k, n, in_bytes):
    return pl.CostEstimate(flops=6 * m * k * n, bytes_accessed=in_bytes, transcendentals=0)


def after(x, *others):
    return lax.optimization_barrier((x, *others))[0]


def step(x):
    return lax.ppermute(x, ROW, [(2 * i + c, 2 * ((i + 1 - 2 * c) % 4) + c) for i in range(4) for c in range(2)])


def swap(x):
    return lax.ppermute(x, "core", [(0, 1), (1, 0)])


def gather_rows(x):
    mine = [x]
    for _ in range(3):
        mine.append(step(mine[-1]))
    return mine + [swap(t) for t in mine]


def hop(x, along, by):
    pairs = []
    for core in range(2):
        for i in range(4):
            for j in range(4):
                to = (i, (j + by) % 4) if along == core else ((i + by) % 4, j)
                pairs.append((16 * core + 4 * i + j, 16 * core + 4 * to[0] + to[1]))
    return lax.ppermute(x, ("core",) + COL, pairs)


def gather_cols(x, axis, gates=((), (), ())):
    half = x.shape[axis] // 2
    up, down = hop(x, 0, 1), hop(x, 0, -1)
    top = hop(lax.slice_in_dim(after(up, *gates[0]), 0, half, axis=axis), 0, 1)
    low = hop(lax.slice_in_dim(after(down, *gates[0]), half, 2 * half, axis=axis), 0, -1)
    group = after(jnp.stack([x, up, down, jnp.concatenate([top, low], axis=axis)]), *gates[1])
    up, down = hop(group, 1, 1), hop(group, 1, -1)
    return (group, up, down), (hop(after(up, *gates[2])[:2], 1, 1), hop(after(down, *gates[2])[2:], 1, -1))


def places():
    y, core, z, x = (lax.axis_index(n) for n in ALL)
    s = 1 - 2 * core
    near = lambda i, k: lax.rem(i + k + 8, 4)
    rows = [2 * near(y, -s * k) + core for k in range(4)] + [2 * near(y, s * k) + 1 - core for k in range(4)]
    first, second = jnp.where(core == 0, x, z), jnp.where(core == 0, z, x)
    cols = []
    for k in (0, -1, 1, 2):
        for i in (0, -1, 1, 2):
            u, v = near(first, i), near(second, k)
            cols.append(jnp.where(core == 0, 4 * v + u, 4 * u + v))
    return jnp.stack(rows + cols).astype(jnp.int32)


def dot3(a, b):
    a_hi, b_hi = a.astype(jnp.bfloat16), b.astype(jnp.bfloat16)
    a_lo = (a - a_hi.astype(F32)).astype(jnp.bfloat16)
    b_lo = (b - b_hi.astype(F32)).astype(jnp.bfloat16)
    mul = lambda p, q: jnp.dot(p, q, preferred_element_type=F32)
    return mul(a_hi, b_hi) + (mul(a_hi, b_lo) + mul(a_lo, b_hi))


def pair_dot(at, tile, a_buf, slot, b_buf, per):
    def one(k):
        return a_buf[slot + k], b_buf[lax.div(at[tile + k], per)]

    def body(q):
        (a0, b0), (a1, b1) = one(q), one(3 - q)
        return dot3(jnp.concatenate([a0, a1], axis=1), jnp.concatenate([b0, b1], axis=0))

    return body


def near_kernel(per, at, *refs):
    groups, tiles, acc, (a_buf, b_buf, a_sem, b_sem) = refs[:3], refs[3], refs[4], refs[5:]
    outs = acc.shape[0]
    copies = [pltpu.make_async_copy(tiles, b_buf, b_sem)]
    copies += [pltpu.make_async_copy(groups[i], a_buf.at[pl.ds(4 * i, 4)], a_sem.at[i]) for i in range(3)]
    for copy in copies:
        copy.start()
    acc[...] = jnp.zeros_like(acc)
    for copy in copies:
        copy.wait()

    def body(i, carry):
        g, q = lax.div(i, 2), lax.rem(i, 2)
        p = lax.rem(at[8 + 4 * g + q], outs)
        acc[p] += pair_dot(at, 8 + 4 * g, a_buf, 4 * g, b_buf, per)(q)
        return carry

    lax.fori_loop(0, 6, body, 0)


def near_product(at, groups, tiles, outs):
    m, w = groups[0].shape[1:]
    many, _, n = tiles.shape
    return pl.pallas_call(
        functools.partial(near_kernel, 16 // many),
        out_shape=jax.ShapeDtypeStruct((outs, m, n), F32),
        in_specs=[SMEM] + [ANY] * 4,
        out_specs=VMEM,
        scratch_shapes=[
            pltpu.VMEM((12, m, w), F32),
            pltpu.VMEM(tiles.shape, F32),
            pltpu.SemaphoreType.DMA((3,)),
            pltpu.SemaphoreType.DMA,
        ],
        compiler_params=params(40),
        cost_estimate=cost(20 * m, 12 * w, n, 20 * 4 * w * (12 * m + many * n)),
        name="near",
    )(at, *groups, tiles)


def far_sum(at, top, low, tiles, a_buf, b_buf, sem, per):
    copies = [pltpu.make_async_copy(top, a_buf.at[pl.ds(0, 2)], sem.at[0])]
    copies += [pltpu.make_async_copy(low, a_buf.at[pl.ds(2, 2)], sem.at[1])]
    copies += [pltpu.make_async_copy(tiles.at[lax.div(at[20 + k], per)], b_buf.at[k], sem.at[2 + k]) for k in range(4)]
    for copy in copies:
        copy.start()
    for copy in copies:
        copy.wait()
    for q in range(2):
        yield q, dot3(
            jnp.concatenate([a_buf[q], a_buf[3 - q]], axis=1), jnp.concatenate([b_buf[q], b_buf[3 - q]], axis=0)
        )


def far_scratch(top, tiles):
    return [
        pltpu.VMEM((4,) + top.shape[1:], F32),
        pltpu.VMEM((4,) + tiles.shape[1:], F32),
        pltpu.SemaphoreType.DMA((6,)),
    ]


def update_kernel(at, acc, top, low, tiles, u, ut, a_buf, b_buf, sem):
    total = acc[0]
    for _, part in far_sum(at, top, low, tiles, a_buf, b_buf, sem, 1):
        total += part
    u[...] = total
    ut[...] = total.T


def update_product(at, acc, top, low, tiles):
    _, m, n = acc.shape
    return pl.pallas_call(
        update_kernel,
        out_shape=(jax.ShapeDtypeStruct((m, n), F32), jax.ShapeDtypeStruct((n, m), F32)),
        in_specs=[SMEM, VMEM, ANY, ANY, ANY],
        out_specs=(VMEM, VMEM),
        scratch_shapes=far_scratch(top, tiles),
        compiler_params=params(24),
        cost_estimate=cost(m, 4 * top.shape[2], n, 16 * m * n),
        name="update",
    )(at, acc, top, low, tiles)


def child_kernel(at, acc, top, low, tiles, base, child, a_buf, b_buf, sem):
    w = acc.shape[1]
    for p in range(2):
        child[pl.ds(p * w, w)] = base[pl.ds(p * w, w)] - acc[p]
    for q, part in far_sum(at, top, low, tiles, a_buf, b_buf, sem, 2):
        p = pl.multiple_of(lax.rem(at[20 + q], 2) * w, 8)
        child[pl.ds(p, w)] -= part


def child_product(at, acc, top, low, tiles, base):
    return pl.pallas_call(
        child_kernel,
        out_shape=jax.ShapeDtypeStruct(base.shape, F32),
        in_specs=[SMEM, VMEM, ANY, ANY, ANY, VMEM],
        out_specs=VMEM,
        scratch_shapes=far_scratch(top, tiles),
        compiler_params=params(24),
        cost_estimate=cost(acc.shape[1], 4 * top.shape[2], acc.shape[2], 24 * acc.shape[1] * acc.shape[2]),
        name="child",
    )(at, acc, top, low, tiles, base)


def cross_kernel(at, s, *refs):
    tiles, (sigma, u_buf, u_sem) = refs[:8], refs[8:]
    copies = [pltpu.make_async_copy(tiles[i], u_buf.at[:, at[i]], u_sem.at[i]) for i in range(8)]
    for copy in copies:
        copy.start()
    sigma[...] = jnp.zeros_like(sigma)
    for copy in copies:
        copy.wait()
    w = sigma.shape[1]

    def body(k, carry):
        lhs = s[:, pl.ds(pl.multiple_of(k * 768, 128), 768)]
        rhs = u_buf[pl.ds(3 * k, 3)].reshape(768, w)
        sigma[...] -= dot3(lhs, rhs)
        return carry

    lax.fori_loop(0, 4, body, 0)


def cross_product(at, s, tiles):
    m, width = s.shape
    sub, w = tiles[0].shape[1:]
    return pl.pallas_call(
        cross_kernel,
        out_shape=jax.ShapeDtypeStruct((m, w), F32),
        in_specs=[SMEM, VMEM] + [ANY] * 8,
        out_specs=VMEM,
        scratch_shapes=[pltpu.VMEM((NANC, 8, sub, w), F32), pltpu.SemaphoreType.DMA((8,))],
        compiler_params=params(40),
        cost_estimate=cost(m, width, w, 4 * width * (m + w)),
        name="cross",
    )(at, s, *tiles)


def spread(x):
    h, w = x.shape
    sub = h // 24
    return lax.all_to_all(x.reshape(3, 8, sub, w), ROW, 1, 0, tiled=True).reshape(NB, sub, w)


def pick_rows_kernel(anc, x, out):
    for i in range(NANC):
        out[i] = x[anc[i]]


def pick_rows(ancestors, x):
    sub, w = x.shape[1:]
    return pl.pallas_call(
        pick_rows_kernel,
        out_shape=jax.ShapeDtypeStruct((NANC, sub, w), F32),
        in_specs=[SMEM, VMEM],
        out_specs=VMEM,
        compiler_params=params(8),
        name="pick_rows",
    )(ancestors, x).reshape(NANC * sub, w)


def pick_cols_kernel(anc, x, out):
    for i in range(NANC):
        for k in range(2):
            t = 2 * anc[i] + k
            off = pl.multiple_of(lax.rem(t, 3) * 128, 128)
            out[:, pl.ds(i * 256 + k * 128, 128)] = x[lax.div(t, 3), :, pl.ds(off, 128)]


def pick_cols(ancestors, x):
    return pl.pallas_call(
        pick_cols_kernel,
        out_shape=jax.ShapeDtypeStruct((x.shape[1], NANC * 256), F32),
        in_specs=[SMEM, VMEM],
        out_specs=VMEM,
        compiler_params=params(8),
        name="pick_cols",
    )(ancestors, x)


def place_kernel(anc, x, out):
    out[...] = jnp.zeros_like(out)
    for i in range(NANC):
        out[anc[i]] = x[i]


def place_rows(ancestors, x):
    sub, w = x.shape[1:]
    return pl.pallas_call(
        place_kernel,
        out_shape=jax.ShapeDtypeStruct((NB, sub, w), F32),
        in_specs=[SMEM, VMEM],
        out_specs=VMEM,
        compiler_params=params(8),
        name="place_rows",
    )(ancestors, x)


def per_device(sigma_top, factor_cross, factor_inverse, block_inverse, ancestors):
    h, w = sigma_top.shape
    sub = h // 24
    at = places()

    f = pick_rows(ancestors, spread(factor_cross))
    inverse = lax.all_gather(after(factor_inverse, f), ROW, axis=0, tiled=True).reshape(16, w, w)
    f_near, f_far = gather_cols(f, 0)

    s = pick_rows(ancestors, spread(after(sigma_top, f)))
    s = lax.all_to_all(after(s, f_near[0]).reshape(16, -1, w), COL, 0, 0, tiled=True)
    s_all = lax.all_gather(pick_cols(ancestors, s), COL, axis=0, tiled=True)

    acc = near_product(at, f_near, inverse, 1)
    u, ut = update_product(at, acc, *f_far, inverse)

    moved = lax.ppermute(ut, ALL, [(16 * r + c, 16 * (c // 2) + 2 * r + c % 2) for r in range(8) for c in range(16)])
    u_near, u_far = gather_cols(moved, 0)
    u_tiles = gather_rows(u.reshape(NANC, sub, w))

    sigma = cross_product(at, after(s_all, u_near[0]), u_tiles)
    sigma_all = lax.all_gather(sigma, ROW, axis=0, tiled=True).reshape(8, w, w)
    acc = near_product(at, u_near, sigma_all, 2)
    sigma_child = child_product(at, acc, *u_far, sigma_all, block_inverse)

    full = place_rows(ancestors, sigma.reshape(NANC, sub, w))
    back = lax.all_to_all(full.reshape(8, 3, sub, w), ROW, 0, 0, tiled=True)
    sigma_cross = back.reshape(8, 3, sub, w).transpose(1, 0, 2, 3).reshape(h, w)
    return (sigma_cross, sigma_child)


def solution(mesh):
    fine = Mesh(np.asarray(mesh.devices).reshape(4, 2, 4, 4), ALL)
    tile = P(ROW, COL)
    return jax.shard_map(
        per_device,
        mesh=fine,
        in_specs=(tile, tile, tile, tile, P()),
        out_specs=(tile, tile),
        check_vma=False,
    )
```

```python
import functools

import jax
import jax.numpy as jnp
import numpy as np
from jax import lax
from jax.experimental import pallas as pl
from jax.experimental.pallas import tpu as pltpu
from jax.sharding import Mesh, PartitionSpec as P

NB = 24
NANC = 12
W1, W2 = 12, 12
ROW = ("y", "core")
COL = ("z", "x")
ALL = ("y", "core", "z", "x")
VMEM = pl.BlockSpec(memory_space=pltpu.VMEM)
SMEM = pl.BlockSpec(memory_space=pltpu.SMEM)
ANY = pl.BlockSpec(memory_space=pl.ANY)
F32 = jnp.float32


def params(mib):
    return pltpu.CompilerParams(vmem_limit_bytes=mib * 1024 * 1024)


def cost(m, k, n, in_bytes):
    return pl.CostEstimate(flops=6 * m * k * n, bytes_accessed=in_bytes, transcendentals=0)


def after(x, *others):
    return lax.optimization_barrier((x, *others))[0]


def step(x):
    return lax.ppermute(x, ROW, [(2 * i + c, 2 * ((i + 1 - 2 * c) % 4) + c) for i in range(4) for c in range(2)])


def swap(x):
    return lax.ppermute(x, "core", [(0, 1), (1, 0)])


def gather_rows(x):
    mine = [x]
    for _ in range(3):
        mine.append(step(mine[-1]))
    return mine + [swap(t) for t in mine]


def hop(x, along, by):
    pairs = []
    for core in range(2):
        for i in range(4):
            for j in range(4):
                to = (i, (j + by) % 4) if along == core else ((i + by) % 4, j)
                pairs.append((16 * core + 4 * i + j, 16 * core + 4 * to[0] + to[1]))
    return lax.ppermute(x, ("core",) + COL, pairs)


def gather_cols(x, axis, gates=((), (), ())):
    half = x.shape[axis] // 2
    up, down = hop(x, 0, 1), hop(x, 0, -1)
    top = hop(lax.slice_in_dim(after(up, *gates[0]), 0, half, axis=axis), 0, 1)
    low = hop(lax.slice_in_dim(after(down, *gates[0]), half, 2 * half, axis=axis), 0, -1)
    group = after(jnp.stack([x, up, down, jnp.concatenate([top, low], axis=axis)]), *gates[1])
    up, down = hop(group, 1, 1), hop(group, 1, -1)
    return (group, up, down), (hop(after(up, *gates[2])[:2], 1, 1), hop(after(down, *gates[2])[2:], 1, -1))


def places():
    y, core, z, x = (lax.axis_index(n) for n in ALL)
    s = 1 - 2 * core
    near = lambda i, k: lax.rem(i + k + 8, 4)
    rows = [2 * near(y, -s * k) + core for k in range(4)] + [2 * near(y, s * k) + 1 - core for k in range(4)]
    first, second = jnp.where(core == 0, x, z), jnp.where(core == 0, z, x)
    cols = []
    for k in (0, -1, 1, 2):
        for i in (0, -1, 1, 2):
            u, v = near(first, i), near(second, k)
            cols.append(jnp.where(core == 0, 4 * v + u, 4 * u + v))
    return jnp.stack(rows + cols).astype(jnp.int32)


def dot3(a, b):
    a_hi, b_hi = a.astype(jnp.bfloat16), b.astype(jnp.bfloat16)
    a_lo = (a - a_hi.astype(F32)).astype(jnp.bfloat16)
    b_lo = (b - b_hi.astype(F32)).astype(jnp.bfloat16)
    mul = lambda p, q: jnp.dot(p, q, preferred_element_type=F32)
    return mul(a_hi, b_hi) + (mul(a_hi, b_lo) + mul(a_lo, b_hi))


def near_kernel(per, at, *refs):
    groups, tiles, acc, (a_buf, b_buf, a_sem, b_sem) = refs[:3], refs[3], refs[4], refs[5:]
    outs = acc.shape[0]

    def group_copy(g, source):
        return pltpu.make_async_copy(source, a_buf.at[pl.ds(4 * g, 4)], a_sem.at[g])

    def tile_copy(k):
        return pltpu.make_async_copy(tiles.at[lax.div(at[8 + k], per)], b_buf.at[k], b_sem.at[k])

    for g in range(3):
        group_copy(g, groups[g]).start()
        for k in (0, 3, 1, 2):
            tile_copy(4 * g + k).start()
    acc[...] = jnp.zeros_like(acc)

    def body(i, carry):
        g, q = lax.div(i, 2), lax.rem(i, 2)

        @pl.when(q == 0)
        def _():
            group_copy(g, groups[0]).wait()

        k0, k1 = 4 * g + q, 4 * g + 3 - q
        tile_copy(k0).wait()
        tile_copy(k1).wait()
        acc[lax.rem(at[8 + k0], outs)] += dot3(
            jnp.concatenate([a_buf[k0], a_buf[k1]], axis=1), jnp.concatenate([b_buf[k0], b_buf[k1]], axis=0)
        )
        return carry

    lax.fori_loop(0, 6, body, 0)


def near_product(at, groups, tiles, outs, weight):
    m, w = groups[0].shape[1:]
    many, _, n = tiles.shape
    return pl.pallas_call(
        functools.partial(near_kernel, 16 // many),
        out_shape=jax.ShapeDtypeStruct((outs, m, n), F32),
        in_specs=[SMEM] + [ANY] * 4,
        out_specs=VMEM,
        scratch_shapes=[
            pltpu.VMEM((12, m, w), F32),
            pltpu.VMEM((12,) + tiles.shape[1:], F32),
            pltpu.SemaphoreType.DMA((3,)),
            pltpu.SemaphoreType.DMA((12,)),
        ],
        compiler_params=params(40),
        cost_estimate=cost(weight * m, 12 * w, n, weight * 4 * w * (12 * m + many * n)),
        name="near",
    )(at, *groups, tiles)


def far_sum(at, top, low, tiles, a_buf, b_buf, sem, per):
    copies = [pltpu.make_async_copy(top, a_buf.at[pl.ds(0, 2)], sem.at[0])]
    copies += [pltpu.make_async_copy(low, a_buf.at[pl.ds(2, 2)], sem.at[1])]
    copies += [pltpu.make_async_copy(tiles.at[lax.div(at[20 + k], per)], b_buf.at[k], sem.at[2 + k]) for k in range(4)]
    for copy in copies:
        copy.start()
    for copy in copies:
        copy.wait()
    for q in range(2):
        yield q, dot3(
            jnp.concatenate([a_buf[q], a_buf[3 - q]], axis=1), jnp.concatenate([b_buf[q], b_buf[3 - q]], axis=0)
        )


def far_scratch(top, tiles):
    return [
        pltpu.VMEM((4,) + top.shape[1:], F32),
        pltpu.VMEM((4,) + tiles.shape[1:], F32),
        pltpu.SemaphoreType.DMA((6,)),
    ]


def update_kernel(at, acc, top, low, tiles, u, ut, a_buf, b_buf, sem):
    total = acc[0]
    for _, part in far_sum(at, top, low, tiles, a_buf, b_buf, sem, 1):
        total += part
    u[...] = total
    ut[...] = total.T


def update_product(at, acc, top, low, tiles):
    _, m, n = acc.shape
    return pl.pallas_call(
        update_kernel,
        out_shape=(jax.ShapeDtypeStruct((m, n), F32), jax.ShapeDtypeStruct((n, m), F32)),
        in_specs=[SMEM, VMEM, ANY, ANY, ANY],
        out_specs=(VMEM, VMEM),
        scratch_shapes=far_scratch(top, tiles),
        compiler_params=params(24),
        cost_estimate=cost(m, 4 * top.shape[2], n, 16 * m * n),
        name="update",
    )(at, acc, top, low, tiles)


def child_kernel(at, acc, top, low, tiles, base, child, a_buf, b_buf, sem):
    w = acc.shape[1]
    for p in range(2):
        child[pl.ds(p * w, w)] = base[pl.ds(p * w, w)] - acc[p]
    for q, part in far_sum(at, top, low, tiles, a_buf, b_buf, sem, 2):
        p = pl.multiple_of(lax.rem(at[20 + q], 2) * w, 8)
        child[pl.ds(p, w)] -= part


def child_product(at, acc, top, low, tiles, base):
    return pl.pallas_call(
        child_kernel,
        out_shape=jax.ShapeDtypeStruct(base.shape, F32),
        in_specs=[SMEM, VMEM, ANY, ANY, ANY, VMEM],
        out_specs=VMEM,
        scratch_shapes=far_scratch(top, tiles),
        compiler_params=params(24),
        cost_estimate=cost(acc.shape[1], 4 * top.shape[2], acc.shape[2], 24 * acc.shape[1] * acc.shape[2]),
        name="child",
    )(at, acc, top, low, tiles, base)


def cross_kernel(at, s, *refs):
    tiles, (sigma, u_buf, u_sem) = refs[:8], refs[8:]
    copies = [pltpu.make_async_copy(tiles[i], u_buf.at[:, at[i]], u_sem.at[i]) for i in range(8)]
    for copy in copies:
        copy.start()
    sigma[...] = jnp.zeros_like(sigma)
    for copy in copies:
        copy.wait()
    w = sigma.shape[1]

    def body(k, carry):
        lhs = s[:, pl.ds(pl.multiple_of(k * 768, 128), 768)]
        rhs = u_buf[pl.ds(3 * k, 3)].reshape(768, w)
        sigma[...] -= dot3(lhs, rhs)
        return carry

    lax.fori_loop(0, 4, body, 0)


def cross_product(at, s, tiles):
    m, width = s.shape
    sub, w = tiles[0].shape[1:]
    return pl.pallas_call(
        cross_kernel,
        out_shape=jax.ShapeDtypeStruct((m, w), F32),
        in_specs=[SMEM, VMEM] + [ANY] * 8,
        out_specs=VMEM,
        scratch_shapes=[pltpu.VMEM((NANC, 8, sub, w), F32), pltpu.SemaphoreType.DMA((8,))],
        compiler_params=params(40),
        cost_estimate=cost(m, width, w, 4 * width * (m + w)),
        name="cross",
    )(at, s, *tiles)


def spread(x):
    h, w = x.shape
    sub = h // 24
    return lax.all_to_all(x.reshape(3, 8, sub, w), ROW, 1, 0, tiled=True).reshape(NB, sub, w)


def pick_rows_kernel(anc, x, out):
    for i in range(NANC):
        out[i] = x[anc[i]]


def pick_rows(ancestors, x):
    sub, w = x.shape[1:]
    return pl.pallas_call(
        pick_rows_kernel,
        out_shape=jax.ShapeDtypeStruct((NANC, sub, w), F32),
        in_specs=[SMEM, VMEM],
        out_specs=VMEM,
        compiler_params=params(8),
        name="pick_rows",
    )(ancestors, x).reshape(NANC * sub, w)


def pick_cols_kernel(anc, x, out):
    for i in range(NANC):
        for k in range(2):
            t = 2 * anc[i] + k
            off = pl.multiple_of(lax.rem(t, 3) * 128, 128)
            out[:, pl.ds(i * 256 + k * 128, 128)] = x[lax.div(t, 3), :, pl.ds(off, 128)]


def pick_cols(ancestors, x):
    return pl.pallas_call(
        pick_cols_kernel,
        out_shape=jax.ShapeDtypeStruct((x.shape[1], NANC * 256), F32),
        in_specs=[SMEM, VMEM],
        out_specs=VMEM,
        compiler_params=params(8),
        name="pick_cols",
    )(ancestors, x)


def place_kernel(anc, first, x, out, sem):
    out[...] = jnp.zeros_like(out)
    for b in range(out.shape[0]):
        for i in range(NANC):

            @pl.when(anc[i] == first[0] + b)
            def _():
                copy = pltpu.make_async_copy(x.at[:, i], out.at[b], sem)
                copy.start()
                copy.wait()


def place_rows(ancestors, x, h):
    _, _, sub, w = x.shape
    first = (3 * lax.axis_index(ROW)).astype(jnp.int32).reshape(1)
    return pl.pallas_call(
        place_kernel,
        out_shape=jax.ShapeDtypeStruct((3, 8, sub, w), F32),
        in_specs=[SMEM, SMEM, ANY],
        out_specs=VMEM,
        scratch_shapes=[pltpu.SemaphoreType.DMA],
        compiler_params=params(8),
        name="place_rows",
    )(ancestors, first, x).reshape(h, w)


def per_device(sigma_top, factor_cross, factor_inverse, block_inverse, ancestors):
    h, w = sigma_top.shape
    sub = h // 24
    at = places()

    f = pick_rows(ancestors, spread(factor_cross))
    inverse = lax.all_gather(after(factor_inverse, f), ROW, axis=0, tiled=True).reshape(16, w, w)
    f_near, f_far = gather_cols(f, 0)

    s = pick_rows(ancestors, spread(after(sigma_top, f)))
    s = lax.all_to_all(after(s, f_near[0]).reshape(16, -1, w), COL, 0, 0, tiled=True)
    s_all = lax.all_gather(pick_cols(ancestors, s), COL, axis=0, tiled=True)

    acc = near_product(at, f_near, inverse, 1, W1)
    u, ut = update_product(at, acc, *f_far, inverse)

    moved = lax.ppermute(ut, ALL, [(16 * r + c, 16 * (c // 2) + 2 * r + c % 2) for r in range(8) for c in range(16)])
    u_near, u_far = gather_cols(moved, 0)
    u_tiles = gather_rows(u.reshape(NANC, sub, w))

    sigma = cross_product(at, after(s_all, u_near[0]), u_tiles)
    sigma_all = lax.all_gather(sigma, ROW, axis=0, tiled=True).reshape(8, w, w)
    acc = near_product(at, u_near, sigma_all, 2, W2)
    sigma_child = child_product(at, acc, *u_far, sigma_all, block_inverse)

    sigma_cross = place_rows(ancestors, sigma_all.reshape(8, NANC, sub, w), h)
    return (sigma_cross, sigma_child)


def solution(mesh):
    fine = Mesh(np.asarray(mesh.devices).reshape(4, 2, 4, 4), ALL)
    tile = P(ROW, COL)
    return jax.shard_map(
        per_device,
        mesh=fine,
        in_specs=(tile, tile, tile, tile, P()),
        out_specs=(tile, tile),
        check_vma=False,
    )
```

```python
import functools

import jax
import jax.numpy as jnp
import numpy as np
from jax import lax
from jax.experimental import pallas as pl
from jax.experimental.pallas import tpu as pltpu
from jax.sharding import Mesh, PartitionSpec as P

NB = 24
NANC = 12
W1, W2 = 14, 12
ROW = ("y", "core")
COL = ("z", "x")
ALL = ("y", "core", "z", "x")
VMEM = pl.BlockSpec(memory_space=pltpu.VMEM)
SMEM = pl.BlockSpec(memory_space=pltpu.SMEM)
ANY = pl.BlockSpec(memory_space=pl.ANY)
F32 = jnp.float32


def params(mib):
    return pltpu.CompilerParams(vmem_limit_bytes=mib * 1024 * 1024)


def cost(m, k, n, in_bytes):
    return pl.CostEstimate(flops=6 * m * k * n, bytes_accessed=in_bytes, transcendentals=0)


def after(x, *others):
    return lax.optimization_barrier((x, *others))[0]


def step(x):
    return lax.ppermute(x, ROW, [(2 * i + c, 2 * ((i + 1 - 2 * c) % 4) + c) for i in range(4) for c in range(2)])


def swap(x):
    return lax.ppermute(x, "core", [(0, 1), (1, 0)])


def gather_rows(x, gate=()):
    mine = [x]
    for k in range(3):
        mine.append(step(after(mine[-1], *gate) if k == 1 else mine[-1]))
    return mine + [swap(t) for t in mine]


def hop(x, along, by):
    pairs = []
    for core in range(2):
        for i in range(4):
            for j in range(4):
                to = (i, (j + by) % 4) if along == core else ((i + by) % 4, j)
                pairs.append((16 * core + 4 * i + j, 16 * core + 4 * to[0] + to[1]))
    return lax.ppermute(x, ("core",) + COL, pairs)


def gather_cols(x, gate=()):
    half = x.shape[0] // 2
    up, down = hop(x, 0, 1), hop(x, 0, -1)
    up, down = lax.optimization_barrier((up, down, *gate))[:2]
    top, low = hop(up[:half], 0, 1), hop(down[half:], 0, -1)
    one, two = jnp.stack([x, up]), jnp.stack([down, jnp.concatenate([top, low])])
    one, two = lax.optimization_barrier((one, two))
    up_one, down_one = hop(one, 1, 1), hop(one, 1, -1)
    up_two, down_two = hop(two, 1, 1), hop(two, 1, -1)
    return (one, two, up_one, up_two, down_one, down_two), (hop(up_one, 1, 1), hop(down_two, 1, -1)), down


def places():
    y, core, z, x = (lax.axis_index(n) for n in ALL)
    s = 1 - 2 * core
    near = lambda i, k: lax.rem(i + k + 8, 4)
    rows = [2 * near(y, -s * k) + core for k in range(4)] + [2 * near(y, s * k) + 1 - core for k in range(4)]
    first, second = jnp.where(core == 0, x, z), jnp.where(core == 0, z, x)
    cols = []
    for k in (0, -1, 1, 2):
        for i in (0, -1, 1, 2):
            u, v = near(first, i), near(second, k)
            cols.append(jnp.where(core == 0, 4 * v + u, 4 * u + v))
    return jnp.stack(rows + cols).astype(jnp.int32)


def dot3(a, b):
    a_hi, b_hi = a.astype(jnp.bfloat16), b.astype(jnp.bfloat16)
    a_lo = (a - a_hi.astype(F32)).astype(jnp.bfloat16)
    b_lo = (b - b_hi.astype(F32)).astype(jnp.bfloat16)
    mul = lambda p, q: jnp.dot(p, q, preferred_element_type=F32)
    return mul(a_hi, b_hi) + (mul(a_hi, b_lo) + mul(a_lo, b_hi))


def pair_copy(a_buf, a_sem, i, source):
    return pltpu.make_async_copy(source, a_buf.at[pl.ds(2 * i, 2)], a_sem.at[i])


def near_rows_kernel(at, *refs):
    pairs, tiles, (acc, far), (a_buf, b_buf, a_sem, b_sem) = refs[:6], refs[6:14], refs[14:16], refs[16:]
    copies = [pltpu.make_async_copy(tiles[i], b_buf.at[pl.ds(2 * at[i], 2)], b_sem.at[i]) for i in range(8)]
    copies += [pair_copy(a_buf, a_sem, i, pairs[i]) for i in range(6)]
    for copy in copies:
        copy.start()
    acc[...] = jnp.zeros_like(acc)
    for copy in copies:
        copy.wait()

    def body(i, carry):
        k0 = 4 * lax.div(i, 2) + lax.rem(i, 2)
        k1 = k0 + 3 - 2 * lax.rem(i, 2)
        acc[0] += dot3(
            jnp.concatenate([a_buf[k0], a_buf[k1]], axis=1),
            jnp.concatenate([b_buf[at[8 + k0]], b_buf[at[8 + k1]]], axis=0),
        )
        return carry

    lax.fori_loop(0, 6, body, 0)
    for k in range(4):
        far[k] = b_buf[at[20 + k]]


def near_rows_product(at, pairs, tiles):
    m, w = pairs[0].shape[1:]
    _, k, n = tiles[0].shape
    return pl.pallas_call(
        near_rows_kernel,
        out_shape=(jax.ShapeDtypeStruct((1, m, n), F32), jax.ShapeDtypeStruct((4, k, n), F32)),
        in_specs=[SMEM] + [ANY] * 14,
        out_specs=(VMEM, VMEM),
        scratch_shapes=[
            pltpu.VMEM((12, m, w), F32),
            pltpu.VMEM((16, k, n), F32),
            pltpu.SemaphoreType.DMA((6,)),
            pltpu.SemaphoreType.DMA((8,)),
        ],
        compiler_params=params(40),
        cost_estimate=cost(W1 * m, 12 * w, n, W1 * 4 * w * (12 * m + 16 * n)),
        name="near_rows",
    )(at, *pairs, *tiles)


def near_kernel(at, *refs):
    pairs, tiles, acc, (a_buf, b_buf, a_sem, b_sem) = refs[:6], refs[6], refs[7], refs[8:]
    outs = acc.shape[0]

    def tile_copy(k):
        return pltpu.make_async_copy(tiles.at[lax.div(at[8 + k], 2)], b_buf.at[k], b_sem.at[k])

    for i in range(6):
        pair_copy(a_buf, a_sem, i, pairs[i]).start()
        tile_copy(2 * i).start()
        tile_copy(2 * i + 1).start()
    acc[...] = jnp.zeros_like(acc)

    def body(i, carry):
        g, q = lax.div(i, 2), lax.rem(i, 2)

        @pl.when(q == 0)
        def _():
            for k in range(2):
                pair_copy(a_buf, a_sem, 2 * g + k, pairs[0]).wait()

        k0, k1 = 4 * g + q, 4 * g + 3 - q
        tile_copy(k0).wait()
        tile_copy(k1).wait()
        acc[lax.rem(at[8 + k0], outs)] += dot3(
            jnp.concatenate([a_buf[k0], a_buf[k1]], axis=1), jnp.concatenate([b_buf[k0], b_buf[k1]], axis=0)
        )
        return carry

    lax.fori_loop(0, 6, body, 0)


def near_product(at, pairs, tiles):
    m, w = pairs[0].shape[1:]
    many, _, n = tiles.shape
    return pl.pallas_call(
        near_kernel,
        out_shape=jax.ShapeDtypeStruct((2, m, n), F32),
        in_specs=[SMEM] + [ANY] * 7,
        out_specs=VMEM,
        scratch_shapes=[
            pltpu.VMEM((12, m, w), F32),
            pltpu.VMEM((12,) + tiles.shape[1:], F32),
            pltpu.SemaphoreType.DMA((6,)),
            pltpu.SemaphoreType.DMA((12,)),
        ],
        compiler_params=params(40),
        cost_estimate=cost(W2 * m, 12 * w, n, W2 * 4 * w * (12 * m + many * n)),
        name="near",
    )(at, *pairs, tiles)


def far_sum(at, top, low, tiles, a_buf, b_buf, sem, per):
    copies = [pltpu.make_async_copy(top, a_buf.at[pl.ds(0, 2)], sem.at[0])]
    copies += [pltpu.make_async_copy(low, a_buf.at[pl.ds(2, 2)], sem.at[1])]
    index = lambda k: lax.div(at[20 + k], per) if per else k
    copies += [pltpu.make_async_copy(tiles.at[index(k)], b_buf.at[k], sem.at[2 + k]) for k in range(4)]
    for copy in copies:
        copy.start()
    for copy in copies:
        copy.wait()
    for q in range(2):
        yield q, dot3(
            jnp.concatenate([a_buf[q], a_buf[3 - q]], axis=1), jnp.concatenate([b_buf[q], b_buf[3 - q]], axis=0)
        )


def far_scratch(top, tiles):
    return [
        pltpu.VMEM((4,) + top.shape[1:], F32),
        pltpu.VMEM((4,) + tiles.shape[1:], F32),
        pltpu.SemaphoreType.DMA((6,)),
    ]


def update_kernel(at, acc, top, low, tiles, u, ut, a_buf, b_buf, sem):
    total = acc[0]
    for _, part in far_sum(at, top, low, tiles, a_buf, b_buf, sem, 0):
        total += part
    u[...] = total
    ut[...] = total.T


def update_product(at, acc, top, low, tiles):
    _, m, n = acc.shape
    return pl.pallas_call(
        update_kernel,
        out_shape=(jax.ShapeDtypeStruct((m, n), F32), jax.ShapeDtypeStruct((n, m), F32)),
        in_specs=[SMEM, VMEM, ANY, ANY, ANY],
        out_specs=(VMEM, VMEM),
        scratch_shapes=far_scratch(top, tiles),
        compiler_params=params(24),
        cost_estimate=cost(m, 4 * top.shape[2], n, 16 * m * n),
        name="update",
    )(at, acc, top, low, tiles)


def child_kernel(at, acc, top, low, tiles, base, child, a_buf, b_buf, sem):
    w = acc.shape[1]
    for p in range(2):
        child[pl.ds(p * w, w)] = base[pl.ds(p * w, w)] - acc[p]
    for q, part in far_sum(at, top, low, tiles, a_buf, b_buf, sem, 2):
        p = pl.multiple_of(lax.rem(at[20 + q], 2) * w, 8)
        child[pl.ds(p, w)] -= part


def child_product(at, acc, top, low, tiles, base):
    return pl.pallas_call(
        child_kernel,
        out_shape=jax.ShapeDtypeStruct(base.shape, F32),
        in_specs=[SMEM, VMEM, ANY, ANY, ANY, VMEM],
        out_specs=VMEM,
        scratch_shapes=far_scratch(top, tiles),
        compiler_params=params(24),
        cost_estimate=cost(acc.shape[1], 4 * top.shape[2], acc.shape[2], 24 * acc.shape[1] * acc.shape[2]),
        name="child",
    )(at, acc, top, low, tiles, base)


def cross_kernel(s, u, sigma, u_buf, u_sem):
    copies = [pltpu.make_async_copy(u.at[i], u_buf.at[:, i], u_sem.at[i]) for i in range(8)]
    for copy in copies:
        copy.start()
    sigma[...] = jnp.zeros_like(sigma)
    for copy in copies:
        copy.wait()
    w = sigma.shape[1]

    def body(k, carry):
        lhs = s[:, pl.ds(pl.multiple_of(k * 768, 128), 768)]
        rhs = u_buf[pl.ds(3 * k, 3)].reshape(768, w)
        sigma[...] -= dot3(lhs, rhs)
        return carry

    lax.fori_loop(0, 4, body, 0)


def cross_product(s, u):
    m, width = s.shape
    _, _, sub, w = u.shape
    return pl.pallas_call(
        cross_kernel,
        out_shape=jax.ShapeDtypeStruct((m, w), F32),
        in_specs=[VMEM, ANY],
        out_specs=VMEM,
        scratch_shapes=[pltpu.VMEM((NANC, 8, sub, w), F32), pltpu.SemaphoreType.DMA((8,))],
        compiler_params=params(40),
        cost_estimate=cost(m, width, w, 4 * width * (m + w)),
        name="cross",
    )(s, u)


def spread(x):
    h, w = x.shape
    sub = h // 24
    return lax.all_to_all(x.reshape(3, 8, sub, w), ROW, 1, 0, tiled=True).reshape(NB, sub, w)


def pick_rows_kernel(anc, x, a, b):
    w = a.shape[2]
    for i in range(NANC):
        a[i] = x[anc[i], :, :w]
        b[i] = x[anc[i], :, w:]


def pick_rows(ancestors, x):
    sub, w = x.shape[1], x.shape[2] // 2
    out = jax.ShapeDtypeStruct((NANC, sub, w), F32)
    a, b = pl.pallas_call(
        pick_rows_kernel,
        out_shape=(out, out),
        in_specs=[SMEM, VMEM],
        out_specs=(VMEM, VMEM),
        compiler_params=params(12),
        name="pick_rows",
    )(ancestors, x)
    return a.reshape(NANC * sub, w), b.reshape(NANC * sub, w)


def pick_cols_kernel(anc, x, out):
    for i in range(NANC):
        for k in range(2):
            t = 2 * anc[i] + k
            off = pl.multiple_of(lax.rem(t, 3) * 128, 128)
            out[:, pl.ds(i * 256 + k * 128, 128)] = x[lax.div(t, 3), :, pl.ds(off, 128)]


def pick_cols(ancestors, x):
    return pl.pallas_call(
        pick_cols_kernel,
        out_shape=jax.ShapeDtypeStruct((x.shape[1], NANC * 256), F32),
        in_specs=[SMEM, VMEM],
        out_specs=VMEM,
        compiler_params=params(8),
        name="pick_cols",
    )(ancestors, x)


def place_kernel(anc, first, x, out, sem):
    out[...] = jnp.zeros_like(out)
    for b in range(out.shape[0]):
        for i in range(NANC):

            @pl.when(anc[i] == first[0] + b)
            def _():
                copy = pltpu.make_async_copy(x.at[:, i], out.at[b], sem)
                copy.start()
                copy.wait()


def place_rows(ancestors, x, h):
    _, _, sub, w = x.shape
    first = (3 * lax.axis_index(ROW)).astype(jnp.int32).reshape(1)
    return pl.pallas_call(
        place_kernel,
        out_shape=jax.ShapeDtypeStruct((3, 8, sub, w), F32),
        in_specs=[SMEM, SMEM, ANY],
        out_specs=VMEM,
        scratch_shapes=[pltpu.SemaphoreType.DMA],
        compiler_params=params(8),
        name="place_rows",
    )(ancestors, first, x).reshape(h, w)


def per_device(sigma_top, factor_cross, factor_inverse, block_inverse, ancestors):
    h, w = sigma_top.shape
    sub = h // 24
    at = places()

    both = jnp.concatenate([factor_cross, sigma_top], axis=1)
    f, s = pick_rows(ancestors, spread(both))
    s = pick_cols(ancestors, lax.all_to_all(s.reshape(16, -1, w), COL, 0, 0, tiled=True))
    s_all = lax.all_gather(s, COL, axis=0, tiled=True)
    f_near, f_far, f_down = gather_cols(f, (s,))
    inverse_tiles = [t.reshape(2, w, w) for t in gather_rows(after(factor_inverse, f), (f_down,))]

    acc, far = near_rows_product(at, f_near, inverse_tiles)
    u, ut = update_product(at, acc, *f_far, far)

    moved = lax.ppermute(ut, ALL, [(16 * r + c, 16 * (c // 2) + 2 * r + c % 2) for r in range(8) for c in range(16)])
    u_near, u_far, _ = gather_cols(moved)
    u_all = lax.all_gather(after(u, s_all), ROW, axis=0, tiled=True).reshape(8, NANC, sub, w)

    sigma = cross_product(s_all, after(u_all, u_near[1]))
    sigma_all = lax.all_gather(sigma, ROW, axis=0, tiled=True).reshape(8, w, w)
    acc = near_product(at, u_near, sigma_all)
    sigma_child = child_product(at, acc, *u_far, sigma_all, block_inverse)

    sigma_cross = place_rows(ancestors, sigma_all.reshape(8, NANC, sub, w), h)
    return (sigma_cross, sigma_child)


def solution(mesh):
    fine = Mesh(np.asarray(mesh.devices).reshape(4, 2, 4, 4), ALL)
    tile = P(ROW, COL)
    return jax.shard_map(
        per_device,
        mesh=fine,
        in_specs=(tile, tile, tile, tile, P()),
        out_specs=(tile, tile),
        check_vma=False,
    )
```

```python
import functools

import jax
import jax.numpy as jnp
import numpy as np
from jax import lax
from jax.experimental import pallas as pl
from jax.experimental.pallas import tpu as pltpu
from jax.sharding import Mesh, PartitionSpec as P

NB = 24
NANC = 12
W1, W2 = 18, 12
ROW = ("y", "core")
COL = ("z", "x")
ALL = ("y", "core", "z", "x")
VMEM = pl.BlockSpec(memory_space=pltpu.VMEM)
SMEM = pl.BlockSpec(memory_space=pltpu.SMEM)
ANY = pl.BlockSpec(memory_space=pl.ANY)
F32 = jnp.float32


def params(mib):
    return pltpu.CompilerParams(vmem_limit_bytes=mib * 1024 * 1024)


def cost(m, k, n, in_bytes):
    return pl.CostEstimate(flops=6 * m * k * n, bytes_accessed=in_bytes, transcendentals=0)


def after(x, *others):
    return lax.optimization_barrier((x, *others))[0]


def step(x):
    return lax.ppermute(x, ROW, [(2 * i + c, 2 * ((i + 1 - 2 * c) % 4) + c) for i in range(4) for c in range(2)])


def swap(x):
    return lax.ppermute(x, "core", [(0, 1), (1, 0)])


def gather_rows(x):
    mine = [x]
    for _ in range(3):
        mine.append(step(mine[-1]))
    return mine + [swap(t) for t in mine]


def hop(x, along, by):
    pairs = []
    for core in range(2):
        for i in range(4):
            for j in range(4):
                to = (i, (j + by) % 4) if along == core else ((i + by) % 4, j)
                pairs.append((16 * core + 4 * i + j, 16 * core + 4 * to[0] + to[1]))
    return lax.ppermute(x, ("core",) + COL, pairs)


def gather_cols(x):
    half = x.shape[0] // 2
    up, down = hop(x, 0, 1), hop(x, 0, -1)
    top, low = hop(up[:half], 0, 1), hop(down[half:], 0, -1)
    one, two = jnp.stack([x, up]), jnp.stack([down, jnp.concatenate([top, low])])
    one, two = lax.optimization_barrier((one, two))
    up_one, down_two = hop(one, 1, 1), hop(two, 1, -1)
    up_two, down_one = hop(two, 1, 1), hop(one, 1, -1)
    return (one, two, up_one, up_two, down_one, down_two), (hop(up_one, 1, 1), hop(down_two, 1, -1))


def places():
    y, core, z, x = (lax.axis_index(n) for n in ALL)
    s = 1 - 2 * core
    near = lambda i, k: lax.rem(i + k + 8, 4)
    rows = [2 * near(y, -s * k) + core for k in range(4)] + [2 * near(y, s * k) + 1 - core for k in range(4)]
    first, second = jnp.where(core == 0, x, z), jnp.where(core == 0, z, x)
    cols = []
    for k in (0, -1, 1, 2):
        for i in (0, -1, 1, 2):
            u, v = near(first, i), near(second, k)
            cols.append(jnp.where(core == 0, 4 * v + u, 4 * u + v))
    return jnp.stack(rows + cols).astype(jnp.int32)


def dot3(a, b):
    a_hi, b_hi = a.astype(jnp.bfloat16), b.astype(jnp.bfloat16)
    a_lo = (a - a_hi.astype(F32)).astype(jnp.bfloat16)
    b_lo = (b - b_hi.astype(F32)).astype(jnp.bfloat16)
    mul = lambda p, q: jnp.dot(p, q, preferred_element_type=F32)
    return mul(a_hi, b_hi) + (mul(a_hi, b_lo) + mul(a_lo, b_hi))


def near_kernel(per, at, *refs):
    pairs, tiles, acc, (a_buf, b_buf, a_sem, b_sem) = refs[:6], refs[6], refs[7], refs[8:]
    outs = acc.shape[0]

    def pair_copy(i, source):
        return pltpu.make_async_copy(source, a_buf.at[pl.ds(2 * i, 2)], a_sem.at[i])

    def tile_copy(k):
        return pltpu.make_async_copy(tiles.at[lax.div(at[8 + k], per)], b_buf.at[k], b_sem.at[k])

    for i in range(6):
        pair_copy(i, pairs[i]).start()
        tile_copy(2 * i).start()
        tile_copy(2 * i + 1).start()
    acc[...] = jnp.zeros_like(acc)

    def body(i, carry):
        g, q = lax.div(i, 2), lax.rem(i, 2)

        @pl.when(q == 0)
        def _():
            for k in range(2):
                pair_copy(2 * g + k, pairs[0]).wait()

        k0, k1 = 4 * g + q, 4 * g + 3 - q
        tile_copy(k0).wait()
        tile_copy(k1).wait()
        acc[lax.rem(at[8 + k0], outs)] += dot3(
            jnp.concatenate([a_buf[k0], a_buf[k1]], axis=1), jnp.concatenate([b_buf[k0], b_buf[k1]], axis=0)
        )
        return carry

    lax.fori_loop(0, 6, body, 0)


def near_product(at, pairs, tiles, outs, weight):
    m, w = pairs[0].shape[1:]
    many, _, n = tiles.shape
    return pl.pallas_call(
        functools.partial(near_kernel, 16 // many),
        out_shape=jax.ShapeDtypeStruct((outs, m, n), F32),
        in_specs=[SMEM] + [ANY] * 7,
        out_specs=VMEM,
        scratch_shapes=[
            pltpu.VMEM((12, m, w), F32),
            pltpu.VMEM((12,) + tiles.shape[1:], F32),
            pltpu.SemaphoreType.DMA((6,)),
            pltpu.SemaphoreType.DMA((12,)),
        ],
        compiler_params=params(40),
        cost_estimate=cost(weight * m, 12 * w, n, weight * 4 * w * (12 * m + many * n)),
        name="near",
    )(at, *pairs, tiles)


def far_sum(at, top, low, tiles, a_buf, b_buf, sem, per):
    copies = [pltpu.make_async_copy(top, a_buf.at[pl.ds(0, 2)], sem.at[0])]
    copies += [pltpu.make_async_copy(low, a_buf.at[pl.ds(2, 2)], sem.at[1])]
    copies += [pltpu.make_async_copy(tiles.at[lax.div(at[20 + k], per)], b_buf.at[k], sem.at[2 + k]) for k in range(4)]
    for copy in copies:
        copy.start()
    for copy in copies:
        copy.wait()
    for q in range(2):
        yield q, dot3(
            jnp.concatenate([a_buf[q], a_buf[3 - q]], axis=1), jnp.concatenate([b_buf[q], b_buf[3 - q]], axis=0)
        )


def far_scratch(top, tiles):
    return [
        pltpu.VMEM((4,) + top.shape[1:], F32),
        pltpu.VMEM((4,) + tiles.shape[1:], F32),
        pltpu.SemaphoreType.DMA((6,)),
    ]


def update_kernel(at, acc, top, low, tiles, u, ut, a_buf, b_buf, sem):
    total = acc[0]
    for _, part in far_sum(at, top, low, tiles, a_buf, b_buf, sem, 1):
        total += part
    u[...] = total
    ut[...] = total.T


def update_product(at, acc, top, low, tiles):
    _, m, n = acc.shape
    return pl.pallas_call(
        update_kernel,
        out_shape=(jax.ShapeDtypeStruct((m, n), F32), jax.ShapeDtypeStruct((n, m), F32)),
        in_specs=[SMEM, VMEM, ANY, ANY, ANY],
        out_specs=(VMEM, VMEM),
        scratch_shapes=far_scratch(top, tiles),
        compiler_params=params(24),
        cost_estimate=cost(m, 4 * top.shape[2], n, 16 * m * n),
        name="update",
    )(at, acc, top, low, tiles)


def child_kernel(at, acc, top, low, tiles, base, child, a_buf, b_buf, sem):
    w = acc.shape[1]
    for p in range(2):
        child[pl.ds(p * w, w)] = base[pl.ds(p * w, w)] - acc[p]
    for q, part in far_sum(at, top, low, tiles, a_buf, b_buf, sem, 2):
        p = pl.multiple_of(lax.rem(at[20 + q], 2) * w, 8)
        child[pl.ds(p, w)] -= part


def child_product(at, acc, top, low, tiles, base):
    return pl.pallas_call(
        child_kernel,
        out_shape=jax.ShapeDtypeStruct(base.shape, F32),
        in_specs=[SMEM, VMEM, ANY, ANY, ANY, VMEM],
        out_specs=VMEM,
        scratch_shapes=far_scratch(top, tiles),
        compiler_params=params(24),
        cost_estimate=cost(acc.shape[1], 4 * top.shape[2], acc.shape[2], 24 * acc.shape[1] * acc.shape[2]),
        name="child",
    )(at, acc, top, low, tiles, base)


def cross_kernel(at, s, *refs):
    tiles, (sigma, s_buf, u_buf, s_sem, u_sem) = refs[:8], refs[8:]
    m, w = sigma.shape

    def s_copy(k):
        return pltpu.make_async_copy(s.at[:, pl.ds(768 * k, 768)], s_buf.at[k], s_sem.at[k])

    copies = [pltpu.make_async_copy(tiles[i], u_buf.at[:, at[i]], u_sem.at[i]) for i in range(8)]
    for copy in copies:
        copy.start()
    for k in range(4):
        s_copy(k).start()
    sigma[...] = jnp.zeros_like(sigma)
    for copy in copies:
        copy.wait()
    for k in range(4):
        s_copy(k).wait()
        sigma[...] -= dot3(s_buf[k], u_buf[pl.ds(3 * k, 3)].reshape(768, w))


def cross_product(at, s, tiles):
    m, width = s.shape
    sub, w = tiles[0].shape[1:]
    return pl.pallas_call(
        cross_kernel,
        out_shape=jax.ShapeDtypeStruct((m, w), F32),
        in_specs=[SMEM] + [ANY] * 9,
        out_specs=VMEM,
        scratch_shapes=[
            pltpu.VMEM((4, m, 768), F32),
            pltpu.VMEM((NANC, 8, sub, w), F32),
            pltpu.SemaphoreType.DMA((4,)),
            pltpu.SemaphoreType.DMA((8,)),
        ],
        compiler_params=params(40),
        cost_estimate=cost(m, width, w, 4 * width * (m + w)),
        name="cross",
    )(at, s, *tiles)


def spread(x):
    h, w = x.shape
    sub = h // 24
    return lax.all_to_all(x.reshape(3, 8, sub, w), ROW, 1, 0, tiled=True).reshape(NB, sub, w)


def pick_rows_kernel(anc, x, out):
    for i in range(NANC):
        out[i] = x[anc[i]]


def pick_rows(ancestors, x):
    sub, w = x.shape[1:]
    return pl.pallas_call(
        pick_rows_kernel,
        out_shape=jax.ShapeDtypeStruct((NANC, sub, w), F32),
        in_specs=[SMEM, VMEM],
        out_specs=VMEM,
        compiler_params=params(8),
        name="pick_rows",
    )(ancestors, x).reshape(NANC * sub, w)


def pick_cols_kernel(anc, x, out):
    for i in range(NANC):
        for k in range(2):
            t = 2 * anc[i] + k
            off = pl.multiple_of(lax.rem(t, 3) * 128, 128)
            out[:, pl.ds(i * 256 + k * 128, 128)] = x[lax.div(t, 3), :, pl.ds(off, 128)]


def pick_cols(ancestors, x):
    return pl.pallas_call(
        pick_cols_kernel,
        out_shape=jax.ShapeDtypeStruct((x.shape[1], NANC * 256), F32),
        in_specs=[SMEM, VMEM],
        out_specs=VMEM,
        compiler_params=params(8),
        name="pick_cols",
    )(ancestors, x)


def place_kernel(anc, first, x, out, sem):
    out[...] = jnp.zeros_like(out)
    for b in range(out.shape[0]):
        for i in range(NANC):

            @pl.when(anc[i] == first[0] + b)
            def _():
                copy = pltpu.make_async_copy(x.at[:, i], out.at[b], sem)
                copy.start()
                copy.wait()


def place_rows(ancestors, x, h):
    _, _, sub, w = x.shape
    first = (3 * lax.axis_index(ROW)).astype(jnp.int32).reshape(1)
    return pl.pallas_call(
        place_kernel,
        out_shape=jax.ShapeDtypeStruct((3, 8, sub, w), F32),
        in_specs=[SMEM, SMEM, ANY],
        out_specs=VMEM,
        scratch_shapes=[pltpu.SemaphoreType.DMA],
        compiler_params=params(8),
        name="place_rows",
    )(ancestors, first, x).reshape(h, w)


def per_device(sigma_top, factor_cross, factor_inverse, block_inverse, ancestors):
    h, w = sigma_top.shape
    sub = h // 24
    at = places()

    f = pick_rows(ancestors, spread(factor_cross))
    inverse = lax.all_gather(factor_inverse, ROW, axis=0, tiled=True).reshape(16, w, w)
    f_near, f_far = gather_cols(f)

    s = pick_rows(ancestors, spread(after(sigma_top, f)))
    s = lax.all_to_all(after(s, f_near[0]).reshape(16, -1, w), COL, 0, 0, tiled=True)
    s_all = lax.all_gather(pick_cols(ancestors, s), COL, axis=0, tiled=True)

    acc = near_product(at, f_near, inverse, 1, W1)
    u, ut = update_product(at, acc, *f_far, inverse)

    moved = lax.ppermute(ut, ALL, [(16 * r + c, 16 * (c // 2) + 2 * r + c % 2) for r in range(8) for c in range(16)])
    u_near, u_far = gather_cols(moved)
    u_tiles = gather_rows(u.reshape(NANC, sub, w))

    sigma = cross_product(at, after(s_all, u_near[0]), u_tiles)
    sigma_all = lax.all_gather(after(sigma, u_near[2]), ROW, axis=0, tiled=True).reshape(8, w, w)
    acc = near_product(at, u_near, sigma_all, 2, W2)
    sigma_child = child_product(at, acc, *u_far, sigma_all, block_inverse)

    sigma_cross = place_rows(ancestors, sigma_all.reshape(8, NANC, sub, w), h)
    return (sigma_cross, sigma_child)


def solution(mesh):
    fine = Mesh(np.asarray(mesh.devices).reshape(4, 2, 4, 4), ALL)
    tile = P(ROW, COL)
    return jax.shard_map(
        per_device,
        mesh=fine,
        in_specs=(tile, tile, tile, tile, P()),
        out_specs=(tile, tile),
        check_vma=False,
    )
```

```python
import functools

import jax
import jax.numpy as jnp
import numpy as np
from jax import lax
from jax.experimental import pallas as pl
from jax.experimental.pallas import tpu as pltpu
from jax.sharding import Mesh, PartitionSpec as P

NB = 24
NANC = 12
W1, W2 = 14, 12
ROW = ("y", "core")
COL = ("z", "x")
ALL = ("y", "core", "z", "x")
VMEM = pl.BlockSpec(memory_space=pltpu.VMEM)
SMEM = pl.BlockSpec(memory_space=pltpu.SMEM)
ANY = pl.BlockSpec(memory_space=pl.ANY)
F32 = jnp.float32


def params(mib):
    return pltpu.CompilerParams(vmem_limit_bytes=mib * 1024 * 1024)


def cost(m, k, n, in_bytes):
    return pl.CostEstimate(flops=6 * m * k * n, bytes_accessed=in_bytes, transcendentals=0)


def after(x, *others):
    return lax.optimization_barrier((x, *others))[0]


def step(x):
    return lax.ppermute(x, ROW, [(2 * i + c, 2 * ((i + 1 - 2 * c) % 4) + c) for i in range(4) for c in range(2)])


def swap(x):
    return lax.ppermute(x, "core", [(0, 1), (1, 0)])


def gather_rows(x):
    mine = [x]
    for _ in range(3):
        mine.append(step(mine[-1]))
    return mine + [swap(t) for t in mine]


def hop(x, along, by):
    pairs = []
    for core in range(2):
        for i in range(4):
            for j in range(4):
                to = (i, (j + by) % 4) if along == core else ((i + by) % 4, j)
                pairs.append((16 * core + 4 * i + j, 16 * core + 4 * to[0] + to[1]))
    return lax.ppermute(x, ("core",) + COL, pairs)


def gather_cols(x):
    half = x.shape[0] // 2
    up, down = hop(x, 0, 1), hop(x, 0, -1)
    top, low = hop(up[:half], 0, 1), hop(down[half:], 0, -1)
    one, two = jnp.stack([x, up]), jnp.stack([down, jnp.concatenate([top, low])])
    one, two = lax.optimization_barrier((one, two))
    up_one, down_two = hop(one, 1, 1), hop(two, 1, -1)
    up_two, down_one = hop(two, 1, 1), hop(one, 1, -1)
    return (one, two, up_one, up_two, down_one, down_two), (hop(up_one, 1, 1), hop(down_two, 1, -1))


def places():
    y, core, z, x = (lax.axis_index(n) for n in ALL)
    s = 1 - 2 * core
    near = lambda i, k: lax.rem(i + k + 8, 4)
    rows = [2 * near(y, -s * k) + core for k in range(4)] + [2 * near(y, s * k) + 1 - core for k in range(4)]
    first, second = jnp.where(core == 0, x, z), jnp.where(core == 0, z, x)
    cols = []
    for k in (0, -1, 1, 2):
        for i in (0, -1, 1, 2):
            u, v = near(first, i), near(second, k)
            cols.append(jnp.where(core == 0, 4 * v + u, 4 * u + v))
    return jnp.stack(rows + cols).astype(jnp.int32)


def dot3(a, b):
    a_hi, b_hi = a.astype(jnp.bfloat16), b.astype(jnp.bfloat16)
    a_lo = (a - a_hi.astype(F32)).astype(jnp.bfloat16)
    b_lo = (b - b_hi.astype(F32)).astype(jnp.bfloat16)
    mul = lambda p, q: jnp.dot(p, q, preferred_element_type=F32)
    return mul(a_hi, b_hi) + (mul(a_hi, b_lo) + mul(a_lo, b_hi))


def near_kernel(per, at, *refs):
    pairs, tiles, acc, (a_buf, b_buf, a_sem, b_sem) = refs[:6], refs[6], refs[7], refs[8:]
    outs = acc.shape[0]

    def pair_copy(i, source):
        return pltpu.make_async_copy(source, a_buf.at[pl.ds(2 * i, 2)], a_sem.at[i])

    def tile_copy(k):
        return pltpu.make_async_copy(tiles.at[lax.div(at[8 + k], per)], b_buf.at[k], b_sem.at[k])

    for i in range(6):
        pair_copy(i, pairs[i]).start()
        tile_copy(2 * i).start()
        tile_copy(2 * i + 1).start()
    acc[...] = jnp.zeros_like(acc)

    def body(i, carry):
        g, q = lax.div(i, 2), lax.rem(i, 2)

        @pl.when(q == 0)
        def _():
            for k in range(2):
                pair_copy(2 * g + k, pairs[0]).wait()

        k0, k1 = 4 * g + q, 4 * g + 3 - q
        tile_copy(k0).wait()
        tile_copy(k1).wait()
        acc[lax.rem(at[8 + k0], outs)] += dot3(
            jnp.concatenate([a_buf[k0], a_buf[k1]], axis=1), jnp.concatenate([b_buf[k0], b_buf[k1]], axis=0)
        )
        return carry

    lax.fori_loop(0, 6, body, 0)


def near_product(at, pairs, tiles, outs, weight):
    m, w = pairs[0].shape[1:]
    many, _, n = tiles.shape
    return pl.pallas_call(
        functools.partial(near_kernel, 16 // many),
        out_shape=jax.ShapeDtypeStruct((outs, m, n), F32),
        in_specs=[SMEM] + [ANY] * 7,
        out_specs=VMEM,
        scratch_shapes=[
            pltpu.VMEM((12, m, w), F32),
            pltpu.VMEM((12,) + tiles.shape[1:], F32),
            pltpu.SemaphoreType.DMA((6,)),
            pltpu.SemaphoreType.DMA((12,)),
        ],
        compiler_params=params(40),
        cost_estimate=cost(weight * m, 12 * w, n, weight * 4 * w * (12 * m + many * n)),
        name="near",
    )(at, *pairs, tiles)


def far_sum(at, top, low, tiles, a_buf, b_buf, sem, per):
    copies = [pltpu.make_async_copy(top, a_buf.at[pl.ds(0, 2)], sem.at[0])]
    copies += [pltpu.make_async_copy(low, a_buf.at[pl.ds(2, 2)], sem.at[1])]
    copies += [pltpu.make_async_copy(tiles.at[lax.div(at[20 + k], per)], b_buf.at[k], sem.at[2 + k]) for k in range(4)]
    for copy in copies:
        copy.start()
    for copy in copies:
        copy.wait()
    for q in range(2):
        yield q, dot3(
            jnp.concatenate([a_buf[q], a_buf[3 - q]], axis=1), jnp.concatenate([b_buf[q], b_buf[3 - q]], axis=0)
        )


def far_scratch(top, tiles):
    return [
        pltpu.VMEM((4,) + top.shape[1:], F32),
        pltpu.VMEM((4,) + tiles.shape[1:], F32),
        pltpu.SemaphoreType.DMA((6,)),
    ]


def update_kernel(at, acc, top, low, tiles, u, ut, a_buf, b_buf, sem):
    total = acc[0]
    for _, part in far_sum(at, top, low, tiles, a_buf, b_buf, sem, 1):
        total += part
    u[...] = total
    ut[...] = total.T


def update_product(at, acc, top, low, tiles):
    _, m, n = acc.shape
    return pl.pallas_call(
        update_kernel,
        out_shape=(jax.ShapeDtypeStruct((m, n), F32), jax.ShapeDtypeStruct((n, m), F32)),
        in_specs=[SMEM, VMEM, ANY, ANY, ANY],
        out_specs=(VMEM, VMEM),
        scratch_shapes=far_scratch(top, tiles),
        compiler_params=params(24),
        cost_estimate=cost(m, 4 * top.shape[2], n, 16 * m * n),
        name="update",
    )(at, acc, top, low, tiles)


def child_kernel(at, acc, top, low, tiles, base, child, a_buf, b_buf, sem):
    w = acc.shape[1]
    for p in range(2):
        child[pl.ds(p * w, w)] = base[pl.ds(p * w, w)] - acc[p]
    for q, part in far_sum(at, top, low, tiles, a_buf, b_buf, sem, 2):
        p = pl.multiple_of(lax.rem(at[20 + q], 2) * w, 8)
        child[pl.ds(p, w)] -= part


def child_product(at, acc, top, low, tiles, base):
    return pl.pallas_call(
        child_kernel,
        out_shape=jax.ShapeDtypeStruct(base.shape, F32),
        in_specs=[SMEM, VMEM, ANY, ANY, ANY, VMEM],
        out_specs=VMEM,
        scratch_shapes=far_scratch(top, tiles),
        compiler_params=params(24),
        cost_estimate=cost(acc.shape[1], 4 * top.shape[2], acc.shape[2], 24 * acc.shape[1] * acc.shape[2]),
        name="child",
    )(at, acc, top, low, tiles, base)


def cross_kernel(at, s, *refs):
    tiles, (sigma, s_buf, u_buf, s_sem, u_sem) = refs[:8], refs[8:]
    m, w = sigma.shape

    def s_copy(k):
        return pltpu.make_async_copy(s.at[:, pl.ds(768 * k, 768)], s_buf.at[k], s_sem.at[k])

    copies = [pltpu.make_async_copy(tiles[i], u_buf.at[:, at[i]], u_sem.at[i]) for i in range(8)]
    for copy in copies:
        copy.start()
    for k in range(4):
        s_copy(k).start()
    sigma[...] = jnp.zeros_like(sigma)
    for copy in copies:
        copy.wait()
    for k in range(4):
        s_copy(k).wait()
        sigma[...] -= dot3(s_buf[k], u_buf[pl.ds(3 * k, 3)].reshape(768, w))


def cross_product(at, s, tiles):
    m, width = s.shape
    sub, w = tiles[0].shape[1:]
    return pl.pallas_call(
        cross_kernel,
        out_shape=jax.ShapeDtypeStruct((m, w), F32),
        in_specs=[SMEM] + [ANY] * 9,
        out_specs=VMEM,
        scratch_shapes=[
            pltpu.VMEM((4, m, 768), F32),
            pltpu.VMEM((NANC, 8, sub, w), F32),
            pltpu.SemaphoreType.DMA((4,)),
            pltpu.SemaphoreType.DMA((8,)),
        ],
        compiler_params=params(40),
        cost_estimate=cost(m, width, w, 4 * width * (m + w)),
        name="cross",
    )(at, s, *tiles)


def spread(x):
    h, w = x.shape
    sub = h // 24
    return lax.all_to_all(x.reshape(3, 8, sub, w), ROW, 1, 0, tiled=True).reshape(NB, sub, w)


def pick_rows_kernel(anc, x, out):
    for i in range(NANC):
        out[i] = x[anc[i]]


def pick_rows(ancestors, x):
    sub, w = x.shape[1:]
    return pl.pallas_call(
        pick_rows_kernel,
        out_shape=jax.ShapeDtypeStruct((NANC, sub, w), F32),
        in_specs=[SMEM, VMEM],
        out_specs=VMEM,
        compiler_params=params(8),
        name="pick_rows",
    )(ancestors, x).reshape(NANC * sub, w)


def pick_cols_kernel(anc, x, out):
    for i in range(NANC):
        for k in range(2):
            t = 2 * anc[i] + k
            off = pl.multiple_of(lax.rem(t, 3) * 128, 128)
            out[:, pl.ds(i * 256 + k * 128, 128)] = x[lax.div(t, 3), :, pl.ds(off, 128)]


def pick_cols(ancestors, x):
    return pl.pallas_call(
        pick_cols_kernel,
        out_shape=jax.ShapeDtypeStruct((x.shape[1], NANC * 256), F32),
        in_specs=[SMEM, VMEM],
        out_specs=VMEM,
        compiler_params=params(8),
        name="pick_cols",
    )(ancestors, x)


def place_kernel(anc, first, x, out, sem):
    out[...] = jnp.zeros_like(out)
    for b in range(out.shape[0]):
        for i in range(NANC):

            @pl.when(anc[i] == first[0] + b)
            def _():
                copy = pltpu.make_async_copy(x.at[:, i], out.at[b], sem)
                copy.start()
                copy.wait()


def place_rows(ancestors, x, h):
    _, _, sub, w = x.shape
    first = (3 * lax.axis_index(ROW)).astype(jnp.int32).reshape(1)
    return pl.pallas_call(
        place_kernel,
        out_shape=jax.ShapeDtypeStruct((3, 8, sub, w), F32),
        in_specs=[SMEM, SMEM, ANY],
        out_specs=VMEM,
        scratch_shapes=[pltpu.SemaphoreType.DMA],
        compiler_params=params(8),
        name="place_rows",
    )(ancestors, first, x).reshape(h, w)


def per_device(sigma_top, factor_cross, factor_inverse, block_inverse, ancestors):
    h, w = sigma_top.shape
    sub = h // 24
    at = places()

    f = pick_rows(ancestors, spread(factor_cross))
    inverse = lax.all_gather(factor_inverse, ROW, axis=0, tiled=True).reshape(16, w, w)
    f_near, f_far = gather_cols(f)

    s = pick_rows(ancestors, spread(after(sigma_top, f)))
    s = lax.all_to_all(after(s, f_near[0]).reshape(16, -1, w), COL, 0, 0, tiled=True)
    s_all = lax.all_gather(pick_cols(ancestors, s), COL, axis=0, tiled=True)

    acc = near_product(at, f_near, inverse, 1, W1)
    u, ut = update_product(at, acc, *f_far, inverse)

    moved = lax.ppermute(ut, ALL, [(16 * r + c, 16 * (c // 2) + 2 * r + c % 2) for r in range(8) for c in range(16)])
    u_near, u_far = gather_cols(moved)
    u_tiles = gather_rows(u.reshape(NANC, sub, w))

    sigma = cross_product(at, after(s_all, u_near[0]), u_tiles)
    sigma_all = lax.all_gather(after(sigma, u_near[2]), ROW, axis=0, tiled=True).reshape(8, w, w)
    acc = near_product(at, u_near, sigma_all, 2, W2)
    sigma_child = child_product(at, acc, *u_far, sigma_all, block_inverse)

    sigma_cross = place_rows(ancestors, sigma_all.reshape(8, NANC, sub, w), h)
    return (sigma_cross, sigma_child)


def solution(mesh):
    fine = Mesh(np.asarray(mesh.devices).reshape(4, 2, 4, 4), ALL)
    tile = P(ROW, COL)
    return jax.shard_map(
        per_device,
        mesh=fine,
        in_specs=(tile, tile, tile, tile, P()),
        out_specs=(tile, tile),
        check_vma=False,
    )
```

```python
import functools

import jax
import jax.numpy as jnp
import numpy as np
from jax import lax
from jax.experimental import pallas as pl
from jax.experimental.pallas import tpu as pltpu
from jax.sharding import Mesh, PartitionSpec as P

NB = 24
NANC = 12
W1, W2 = 12, 12
ROW = ("y", "core")
COL = ("z", "x")
ALL = ("y", "core", "z", "x")
VMEM = pl.BlockSpec(memory_space=pltpu.VMEM)
SMEM = pl.BlockSpec(memory_space=pltpu.SMEM)
ANY = pl.BlockSpec(memory_space=pl.ANY)
HBM = pl.BlockSpec(memory_space=pltpu.HBM)
F32 = jnp.float32


def params(mib):
    return pltpu.CompilerParams(vmem_limit_bytes=mib * 1024 * 1024)


def cost(m, k, n, in_bytes):
    return pl.CostEstimate(flops=6 * m * k * n, bytes_accessed=in_bytes, transcendentals=0)


def after(x, *others):
    return lax.optimization_barrier((x, *others))[0]


def step(x):
    return lax.ppermute(x, ROW, [(2 * i + c, 2 * ((i + 1 - 2 * c) % 4) + c) for i in range(4) for c in range(2)])


def swap(x):
    return lax.ppermute(x, "core", [(0, 1), (1, 0)])


def gather_rows(x):
    mine = [x]
    for _ in range(3):
        mine.append(step(mine[-1]))
    return mine + [swap(t) for t in mine]


def hop(x, along, by):
    pairs = []
    for core in range(2):
        for i in range(4):
            for j in range(4):
                to = (i, (j + by) % 4) if along == core else ((i + by) % 4, j)
                pairs.append((16 * core + 4 * i + j, 16 * core + 4 * to[0] + to[1]))
    return lax.ppermute(x, ("core",) + COL, pairs)


def gather_cols(x, whole):
    half = x.shape[0] // 2
    up, down = hop(x, 0, 1), hop(x, 0, -1)
    top, low = hop(up[:half], 0, 1), hop(down[half:], 0, -1)
    if whole:
        group = jnp.stack([x, up, down, jnp.concatenate([top, low])])
        up, down = hop(group, 1, 1), hop(group, 1, -1)
        return (group, up, down), (hop(up[:2], 1, 1), hop(down[2:], 1, -1))
    one, two = jnp.stack([x, up]), jnp.stack([down, jnp.concatenate([top, low])])
    one, two = lax.optimization_barrier((one, two))
    up_one, down_two = hop(one, 1, 1), hop(two, 1, -1)
    up_two, down_one = hop(two, 1, 1), hop(one, 1, -1)
    return (one, two, up_one, up_two, down_one, down_two), (hop(up_one, 1, 1), hop(down_two, 1, -1))


def turn(x):
    at = lambda y, core, z, x: ((2 * y + core) * 4 + z) * 4 + x
    every = [(y, core, z, x) for y in range(4) for core in range(2) for z in range(4) for x in range(4)]
    x = lax.ppermute(x, ALL, [(at(y, c, z, x), at(y, x // 2, (y + z) % 4, 2 * c + x % 2)) for y, c, z, x in every])
    return lax.ppermute(x, ALL, [(at(y, c, z, x), at((z - y) % 4, c, z, x)) for y, c, z, x in every])


def places(turned):
    y, core, z, x = (lax.axis_index(n) for n in ALL)
    s = 1 - 2 * core
    near = lambda i, k: lax.rem(i + k + 8, 4)
    rows = [2 * near(y, -s * k) + core for k in range(4)] + [2 * near(y, s * k) + 1 - core for k in range(4)]
    first, second = jnp.where(core == 0, x, z), jnp.where(core == 0, z, x)
    cols = []
    for k in (0, -1, 1, 2):
        for i in (0, -1, 1, 2):
            u, v = near(first, i), near(second, k)
            at_z, at_x = jnp.where(core == 0, v, u), jnp.where(core == 0, u, v)
            cols.append(4 * (lax.rem(at_z - y + 4, 4) if turned else at_z) + at_x)
    return jnp.stack(rows + cols).astype(jnp.int32)


def dot3(a, b):
    a_hi, b_hi = a.astype(jnp.bfloat16), b.astype(jnp.bfloat16)
    a_lo = (a - a_hi.astype(F32)).astype(jnp.bfloat16)
    b_lo = (b - b_hi.astype(F32)).astype(jnp.bfloat16)
    mul = lambda p, q: jnp.dot(p, q, preferred_element_type=F32)
    return mul(a_hi, b_hi) + (mul(a_hi, b_lo) + mul(a_lo, b_hi))


def near_kernel(per, count, at, *refs):
    pieces, tiles, acc, (a_buf, b_buf, a_sem, b_sem) = refs[:count], refs[count], refs[count + 1], refs[count + 2 :]
    outs, many = acc.shape[0], 12 // count

    def piece_copy(i, source):
        return pltpu.make_async_copy(source, a_buf.at[pl.ds(many * i, many)], a_sem.at[i])

    def tile_copy(k):
        return pltpu.make_async_copy(tiles.at[lax.div(at[8 + k], per)], b_buf.at[k], b_sem.at[k])

    for i in range(count):
        piece_copy(i, pieces[i]).start()
        for k in range(many):
            tile_copy(many * i + k).start()
    acc[...] = jnp.zeros_like(acc)

    def body(i, carry):
        g, q = lax.div(i, 2), lax.rem(i, 2)

        @pl.when(q == 0)
        def _():
            for k in range(count // 3):
                piece_copy((count // 3) * g + k, pieces[0]).wait()

        k0, k1 = 4 * g + q, 4 * g + 3 - q
        tile_copy(k0).wait()
        tile_copy(k1).wait()
        acc[lax.rem(at[8 + k0], outs)] += dot3(
            jnp.concatenate([a_buf[k0], a_buf[k1]], axis=1), jnp.concatenate([b_buf[k0], b_buf[k1]], axis=0)
        )
        return carry

    lax.fori_loop(0, 6, body, 0)


def near_product(at, pieces, tiles, outs, weight):
    m, w = pieces[0].shape[1:]
    many, _, n = tiles.shape
    return pl.pallas_call(
        functools.partial(near_kernel, 16 // many, len(pieces)),
        out_shape=jax.ShapeDtypeStruct((outs, m, n), F32),
        in_specs=[SMEM] + [ANY] * len(pieces) + [HBM],
        out_specs=VMEM,
        scratch_shapes=[
            pltpu.VMEM((12, m, w), F32),
            pltpu.VMEM((12,) + tiles.shape[1:], F32),
            pltpu.SemaphoreType.DMA((len(pieces),)),
            pltpu.SemaphoreType.DMA((12,)),
        ],
        compiler_params=params(40),
        cost_estimate=cost(weight * m, 12 * w, n, weight * 4 * w * (12 * m + many * n)),
        name="near",
    )(at, *pieces, tiles)


def far_sum(at, top, low, tiles, a_buf, b_buf, sem, per):
    copies = [pltpu.make_async_copy(top, a_buf.at[pl.ds(0, 2)], sem.at[0])]
    copies += [pltpu.make_async_copy(low, a_buf.at[pl.ds(2, 2)], sem.at[1])]
    copies += [pltpu.make_async_copy(tiles.at[lax.div(at[20 + k], per)], b_buf.at[k], sem.at[2 + k]) for k in range(4)]
    for copy in copies:
        copy.start()
    for copy in copies:
        copy.wait()
    for q in range(2):
        yield q, dot3(
            jnp.concatenate([a_buf[q], a_buf[3 - q]], axis=1), jnp.concatenate([b_buf[q], b_buf[3 - q]], axis=0)
        )


def far_scratch(top, tiles):
    return [
        pltpu.VMEM((4,) + top.shape[1:], F32),
        pltpu.VMEM((4,) + tiles.shape[1:], F32),
        pltpu.SemaphoreType.DMA((6,)),
    ]


def update_kernel(at, acc, top, low, tiles, u, ut, a_buf, b_buf, sem):
    total = acc[0]
    for _, part in far_sum(at, top, low, tiles, a_buf, b_buf, sem, 1):
        total += part
    u[...] = total
    ut[...] = total.T


def update_product(at, acc, top, low, tiles):
    _, m, n = acc.shape
    return pl.pallas_call(
        update_kernel,
        out_shape=(jax.ShapeDtypeStruct((m, n), F32), jax.ShapeDtypeStruct((n, m), F32)),
        in_specs=[SMEM, VMEM, ANY, ANY, HBM],
        out_specs=(VMEM, VMEM),
        scratch_shapes=far_scratch(top, tiles),
        compiler_params=params(24),
        cost_estimate=cost(m, 4 * top.shape[2], n, 16 * m * n),
        name="update",
    )(at, acc, top, low, tiles)


def child_kernel(at, acc, top, low, tiles, base, child, a_buf, b_buf, sem):
    w = acc.shape[1]
    for p in range(2):
        child[pl.ds(p * w, w)] = base[pl.ds(p * w, w)] - acc[p]
    for q, part in far_sum(at, top, low, tiles, a_buf, b_buf, sem, 2):
        p = pl.multiple_of(lax.rem(at[20 + q], 2) * w, 8)
        child[pl.ds(p, w)] -= part


def child_product(at, acc, top, low, tiles, base):
    return pl.pallas_call(
        child_kernel,
        out_shape=jax.ShapeDtypeStruct(base.shape, F32),
        in_specs=[SMEM, VMEM, ANY, ANY, HBM, VMEM],
        out_specs=VMEM,
        scratch_shapes=far_scratch(top, tiles),
        compiler_params=params(24),
        cost_estimate=cost(acc.shape[1], 4 * top.shape[2], acc.shape[2], 24 * acc.shape[1] * acc.shape[2]),
        name="child",
    )(at, acc, top, low, tiles, base)


def cross_kernel(at, s, *refs):
    tiles, (sigma, s_buf, u_buf, s_sem, u_sem) = refs[:8], refs[8:]
    m, w = sigma.shape

    def s_copy(k):
        return pltpu.make_async_copy(s.at[:, pl.ds(768 * k, 768)], s_buf.at[k], s_sem.at[k])

    copies = [pltpu.make_async_copy(tiles[i], u_buf.at[:, at[i]], u_sem.at[i]) for i in range(8)]
    for copy in copies:
        copy.start()
    for k in range(4):
        s_copy(k).start()
    sigma[...] = jnp.zeros_like(sigma)
    for copy in copies:
        copy.wait()
    for k in range(4):
        s_copy(k).wait()
        sigma[...] -= dot3(s_buf[k], u_buf[pl.ds(3 * k, 3)].reshape(768, w))


def cross_product(at, s, tiles):
    m, width = s.shape
    sub, w = tiles[0].shape[1:]
    return pl.pallas_call(
        cross_kernel,
        out_shape=jax.ShapeDtypeStruct((m, w), F32),
        in_specs=[SMEM, HBM] + [ANY] * 8,
        out_specs=VMEM,
        scratch_shapes=[
            pltpu.VMEM((4, m, 768), F32),
            pltpu.VMEM((NANC, 8, sub, w), F32),
            pltpu.SemaphoreType.DMA((4,)),
            pltpu.SemaphoreType.DMA((8,)),
        ],
        compiler_params=params(40),
        cost_estimate=cost(m, width, w, 4 * width * (m + w)),
        name="cross",
    )(at, s, *tiles)


def spread(x):
    h, w = x.shape
    sub = h // 24
    return lax.all_to_all(x.reshape(3, 8, sub, w), ROW, 1, 0, tiled=True).reshape(NB, sub, w)


def pick_rows_kernel(anc, x, out):
    for i in range(NANC):
        out[i] = x[anc[i]]


def pick_rows(ancestors, x):
    sub, w = x.shape[1:]
    return pl.pallas_call(
        pick_rows_kernel,
        out_shape=jax.ShapeDtypeStruct((NANC, sub, w), F32),
        in_specs=[SMEM, VMEM],
        out_specs=VMEM,
        compiler_params=params(8),
        name="pick_rows",
    )(ancestors, x).reshape(NANC * sub, w)


def pick_cols_kernel(anc, x, out):
    for i in range(NANC):
        for k in range(2):
            t = 2 * anc[i] + k
            off = pl.multiple_of(lax.rem(t, 3) * 128, 128)
            out[:, pl.ds(i * 256 + k * 128, 128)] = x[lax.div(t, 3), :, pl.ds(off, 128)]


def pick_cols(ancestors, x):
    return pl.pallas_call(
        pick_cols_kernel,
        out_shape=jax.ShapeDtypeStruct((x.shape[1], NANC * 256), F32),
        in_specs=[SMEM, VMEM],
        out_specs=VMEM,
        compiler_params=params(8),
        name="pick_cols",
    )(ancestors, x)


def place_kernel(anc, first, x, out, sem):
    out[...] = jnp.zeros_like(out)
    for b in range(out.shape[0]):
        for i in range(NANC):

            @pl.when(anc[i] == first[0] + b)
            def _():
                copy = pltpu.make_async_copy(x.at[:, i], out.at[b], sem)
                copy.start()
                copy.wait()


def place_rows(ancestors, x, h):
    _, _, sub, w = x.shape
    first = (3 * lax.axis_index(ROW)).astype(jnp.int32).reshape(1)
    return pl.pallas_call(
        place_kernel,
        out_shape=jax.ShapeDtypeStruct((3, 8, sub, w), F32),
        in_specs=[SMEM, SMEM, ANY],
        out_specs=VMEM,
        scratch_shapes=[pltpu.SemaphoreType.DMA],
        compiler_params=params(8),
        name="place_rows",
    )(ancestors, first, x).reshape(h, w)


def per_device(sigma_top, factor_cross, factor_inverse, block_inverse, ancestors):
    h, w = sigma_top.shape
    sub = h // 24
    at, at_turned = places(False), places(True)

    f = pick_rows(ancestors, spread(factor_cross))
    inverse = lax.all_gather(after(factor_inverse, f), ROW, axis=0, tiled=True).reshape(16, w, w)
    f_near, f_far = gather_cols(f, True)

    s = pick_rows(ancestors, spread(after(sigma_top, f)))
    s = lax.all_to_all(after(s, f_near[0]).reshape(16, -1, w), COL, 0, 0, tiled=True)
    s_all = lax.all_gather(pick_cols(ancestors, s), COL, axis=0, tiled=True)

    acc = near_product(at, f_near, inverse, 1, W1)
    u, ut = update_product(at, acc, *f_far, inverse)

    u_near, u_far = gather_cols(turn(ut), False)
    u_tiles = gather_rows(u.reshape(NANC, sub, w))

    sigma = cross_product(at, after(s_all, u_near[0]), u_tiles)
    sigma_all = lax.all_gather(sigma, ROW, axis=0, tiled=True).reshape(8, w, w)
    acc = near_product(at_turned, u_near, sigma_all, 2, W2)
    sigma_child = child_product(at_turned, acc, *u_far, sigma_all, block_inverse)

    sigma_cross = place_rows(ancestors, sigma_all.reshape(8, NANC, sub, w), h)
    return (sigma_cross, sigma_child)


def solution(mesh):
    fine = Mesh(np.asarray(mesh.devices).reshape(4, 2, 4, 4), ALL)
    tile = P(ROW, COL)
    return jax.shard_map(
        per_device,
        mesh=fine,
        in_specs=(tile, tile, tile, tile, P()),
        out_specs=(tile, tile),
        check_vma=False,
    )
```

```python
import functools

import jax
import jax.numpy as jnp
import numpy as np
from jax import lax
from jax.experimental import pallas as pl
from jax.experimental.pallas import tpu as pltpu
from jax.sharding import Mesh, PartitionSpec as P

NB = 24
NANC = 12
W1, W2 = 12, 12
ROW = ("y", "core")
COL = ("z", "x")
ALL = ("y", "core", "z", "x")
VMEM = pl.BlockSpec(memory_space=pltpu.VMEM)
SMEM = pl.BlockSpec(memory_space=pltpu.SMEM)
ANY = pl.BlockSpec(memory_space=pl.ANY)
HBM = pl.BlockSpec(memory_space=pltpu.HBM)
F32 = jnp.float32


def params(mib):
    return pltpu.CompilerParams(vmem_limit_bytes=mib * 1024 * 1024)


def cost(m, k, n, in_bytes):
    return pl.CostEstimate(flops=6 * m * k * n, bytes_accessed=in_bytes, transcendentals=0)


def after(x, *others):
    return lax.optimization_barrier((x, *others))[0]


def step(x):
    return lax.ppermute(x, ROW, [(2 * i + c, 2 * ((i + 1 - 2 * c) % 4) + c) for i in range(4) for c in range(2)])


def swap(x):
    return lax.ppermute(x, "core", [(0, 1), (1, 0)])


def gather_rows(x):
    mine = [x]
    for _ in range(3):
        mine.append(step(mine[-1]))
    return mine + [swap(t) for t in mine]


def hop(x, along, by):
    pairs = []
    for core in range(2):
        for i in range(4):
            for j in range(4):
                to = (i, (j + by) % 4) if along == core else ((i + by) % 4, j)
                pairs.append((16 * core + 4 * i + j, 16 * core + 4 * to[0] + to[1]))
    return lax.ppermute(x, ("core",) + COL, pairs)


def gather_cols(x, whole):
    half = x.shape[0] // 2
    up, down = hop(x, 0, 1), hop(x, 0, -1)
    top, low = hop(up[:half], 0, 1), hop(down[half:], 0, -1)
    if whole:
        group = jnp.stack([x, up, down, jnp.concatenate([top, low])])
        up, down = hop(group, 1, 1), hop(group, 1, -1)
        return (group, up, down), (hop(up[:2], 1, 1), hop(down[2:], 1, -1))
    one, two = jnp.stack([x, up]), jnp.stack([down, jnp.concatenate([top, low])])
    one, two = lax.optimization_barrier((one, two))
    up_one, down_two = hop(one, 1, 1), hop(two, 1, -1)
    up_two, down_one = hop(two, 1, 1), hop(one, 1, -1)
    return (one, two, up_one, up_two, down_one, down_two), (hop(up_one, 1, 1), hop(down_two, 1, -1))


def turn(x):
    at = lambda y, core, z, x: ((2 * y + core) * 4 + z) * 4 + x
    every = [(y, core, z, x) for y in range(4) for core in range(2) for z in range(4) for x in range(4)]
    x = lax.ppermute(x, ALL, [(at(y, c, z, x), at(y, x // 2, (y + z) % 4, 2 * c + x % 2)) for y, c, z, x in every])
    return lax.ppermute(x, ALL, [(at(y, c, z, x), at((z - y) % 4, c, z, x)) for y, c, z, x in every])


def places(turned):
    y, core, z, x = (lax.axis_index(n) for n in ALL)
    s = 1 - 2 * core
    near = lambda i, k: lax.rem(i + k + 8, 4)
    rows = [2 * near(y, -s * k) + core for k in range(4)] + [2 * near(y, s * k) + 1 - core for k in range(4)]
    first, second = jnp.where(core == 0, x, z), jnp.where(core == 0, z, x)
    cols = []
    for k in (0, -1, 1, 2):
        for i in (0, -1, 1, 2):
            u, v = near(first, i), near(second, k)
            at_z, at_x = jnp.where(core == 0, v, u), jnp.where(core == 0, u, v)
            cols.append(4 * (lax.rem(at_z - y + 4, 4) if turned else at_z) + at_x)
    return jnp.stack(rows + cols).astype(jnp.int32)


def dot3(a, b):
    a_hi, b_hi = a.astype(jnp.bfloat16), b.astype(jnp.bfloat16)
    a_lo = (a - a_hi.astype(F32)).astype(jnp.bfloat16)
    b_lo = (b - b_hi.astype(F32)).astype(jnp.bfloat16)
    mul = lambda p, q: jnp.dot(p, q, preferred_element_type=F32)
    return mul(a_hi, b_hi) + (mul(a_hi, b_lo) + mul(a_lo, b_hi))


def near_child_kernel(per, count, anc, first, at, *refs):
    tiles, rows, sem = refs[count], refs[count + 2], refs[-1]
    blocks, _, sub, _ = rows.shape
    copies, living = [], []
    for b in range(blocks):
        hits = [jnp.where(anc[i] == first[0] + b, 1, 0) for i in range(NANC)]
        index = sum(i * hit for i, hit in enumerate(hits))
        living.append(sum(hits))
        source = tiles.at[:, pl.ds(pl.multiple_of(index * sub, 8), sub)]
        copies.append(pltpu.make_async_copy(source, rows.at[b], sem.at[b]))
    near_kernel(per, count, at, *refs[: count + 2], *refs[count + 3 : -1], others=copies)
    for b in range(blocks):
        copies[b].wait()

        @pl.when(living[b] == 0)
        def _():
            rows[b] = jnp.zeros_like(rows[b])


def near_kernel(per, count, at, *refs, others=()):
    pieces, tiles, acc, (a_buf, b_buf, a_sem, b_sem) = refs[:count], refs[count], refs[count + 1], refs[count + 2 :]
    outs, many = acc.shape[0], 12 // count

    def piece_copy(i, source):
        return pltpu.make_async_copy(source, a_buf.at[pl.ds(many * i, many)], a_sem.at[i])

    def tile_copy(k):
        return pltpu.make_async_copy(tiles.at[lax.div(at[8 + k], per)], b_buf.at[k], b_sem.at[k])

    for i in range(count):
        piece_copy(i, pieces[i]).start()
        for k in range(many):
            tile_copy(many * i + k).start()
    for copy in others:
        copy.start()
    acc[...] = jnp.zeros_like(acc)

    def body(i, carry):
        g, q = lax.div(i, 2), lax.rem(i, 2)

        @pl.when(q == 0)
        def _():
            for k in range(count // 3):
                piece_copy((count // 3) * g + k, pieces[0]).wait()

        k0, k1 = 4 * g + q, 4 * g + 3 - q
        tile_copy(k0).wait()
        tile_copy(k1).wait()
        acc[lax.rem(at[8 + k0], outs)] += dot3(
            jnp.concatenate([a_buf[k0], a_buf[k1]], axis=1), jnp.concatenate([b_buf[k0], b_buf[k1]], axis=0)
        )
        return carry

    lax.fori_loop(0, 6, body, 0)


def near_product(at, pieces, tiles, outs, weight, ancestors=None):
    m, w = pieces[0].shape[1:]
    many, _, n = tiles.shape
    kernel, extra, out_shape, more = near_kernel, (), [jax.ShapeDtypeStruct((outs, m, n), F32)], []
    if ancestors is not None:
        kernel, extra = near_child_kernel, (ancestors, (3 * lax.axis_index(ROW)).astype(jnp.int32).reshape(1))
        out_shape += [jax.ShapeDtypeStruct((3, many, m // NANC, n), F32)]
        more = [pltpu.SemaphoreType.DMA((3,))]
    return pl.pallas_call(
        functools.partial(kernel, 16 // many, len(pieces)),
        out_shape=out_shape,
        in_specs=[SMEM] * (1 + len(extra)) + [ANY] * len(pieces) + [HBM],
        out_specs=[VMEM] * len(out_shape),
        scratch_shapes=[
            pltpu.VMEM((12, m, w), F32),
            pltpu.VMEM((12,) + tiles.shape[1:], F32),
            pltpu.SemaphoreType.DMA((len(pieces),)),
            pltpu.SemaphoreType.DMA((12,)),
        ] + more,
        compiler_params=params(56),
        cost_estimate=cost(weight * m, 12 * w, n, weight * 4 * w * (12 * m + many * n)),
        name="near",
    )(*extra, at, *pieces, tiles)


def far_sum(at, top, low, tiles, a_buf, b_buf, sem, per):
    copies = [pltpu.make_async_copy(top, a_buf.at[pl.ds(0, 2)], sem.at[0])]
    copies += [pltpu.make_async_copy(low, a_buf.at[pl.ds(2, 2)], sem.at[1])]
    copies += [pltpu.make_async_copy(tiles.at[lax.div(at[20 + k], per)], b_buf.at[k], sem.at[2 + k]) for k in range(4)]
    for copy in copies:
        copy.start()
    for copy in copies:
        copy.wait()
    for q in range(2):
        yield q, dot3(
            jnp.concatenate([a_buf[q], a_buf[3 - q]], axis=1), jnp.concatenate([b_buf[q], b_buf[3 - q]], axis=0)
        )


def far_scratch(top, tiles):
    return [
        pltpu.VMEM((4,) + top.shape[1:], F32),
        pltpu.VMEM((4,) + tiles.shape[1:], F32),
        pltpu.SemaphoreType.DMA((6,)),
    ]


def update_kernel(at, acc, top, low, tiles, u, ut, a_buf, b_buf, sem):
    total = acc[0]
    for _, part in far_sum(at, top, low, tiles, a_buf, b_buf, sem, 1):
        total += part
    u[...] = total
    ut[...] = total.T


def update_product(at, acc, top, low, tiles):
    _, m, n = acc.shape
    return pl.pallas_call(
        update_kernel,
        out_shape=(jax.ShapeDtypeStruct((m, n), F32), jax.ShapeDtypeStruct((n, m), F32)),
        in_specs=[SMEM, VMEM, ANY, ANY, HBM],
        out_specs=(VMEM, VMEM),
        scratch_shapes=far_scratch(top, tiles),
        compiler_params=params(56),
        cost_estimate=cost(m, 4 * top.shape[2], n, 16 * m * n),
        name="update",
    )(at, acc, top, low, tiles)


def child_kernel(at, acc, top, low, tiles, base, child, a_buf, b_buf, sem):
    w = acc.shape[1]
    for p in range(2):
        child[pl.ds(p * w, w)] = base[pl.ds(p * w, w)] - acc[p]
    for q, part in far_sum(at, top, low, tiles, a_buf, b_buf, sem, 2):
        p = pl.multiple_of(lax.rem(at[20 + q], 2) * w, 8)
        child[pl.ds(p, w)] -= part


def child_product(at, acc, top, low, tiles, base):
    return pl.pallas_call(
        child_kernel,
        out_shape=jax.ShapeDtypeStruct(base.shape, F32),
        in_specs=[SMEM, VMEM, ANY, ANY, HBM, VMEM],
        out_specs=VMEM,
        scratch_shapes=far_scratch(top, tiles),
        compiler_params=params(56),
        cost_estimate=cost(acc.shape[1], 4 * top.shape[2], acc.shape[2], 24 * acc.shape[1] * acc.shape[2]),
        name="child",
    )(at, acc, top, low, tiles, base)


def cross_kernel(at, s, *refs):
    tiles, (sigma, s_buf, u_buf, s_sem, u_sem) = refs[:8], refs[8:]
    m, w = sigma.shape

    def s_copy(k):
        return pltpu.make_async_copy(s.at[:, pl.ds(768 * k, 768)], s_buf.at[k], s_sem.at[k])

    copies = [pltpu.make_async_copy(tiles[i], u_buf.at[:, at[i]], u_sem.at[i]) for i in range(8)]
    for copy in copies:
        copy.start()
    for k in range(4):
        s_copy(k).start()
    sigma[...] = jnp.zeros_like(sigma)
    for copy in copies:
        copy.wait()
    for k in range(4):
        s_copy(k).wait()
        sigma[...] -= dot3(s_buf[k], u_buf[pl.ds(3 * k, 3)].reshape(768, w))


def cross_product(at, s, tiles):
    m, width = s.shape
    sub, w = tiles[0].shape[1:]
    return pl.pallas_call(
        cross_kernel,
        out_shape=jax.ShapeDtypeStruct((m, w), F32),
        in_specs=[SMEM, HBM] + [ANY] * 8,
        out_specs=VMEM,
        scratch_shapes=[
            pltpu.VMEM((4, m, 768), F32),
            pltpu.VMEM((NANC, 8, sub, w), F32),
            pltpu.SemaphoreType.DMA((4,)),
            pltpu.SemaphoreType.DMA((8,)),
        ],
        compiler_params=params(56),
        cost_estimate=cost(m, width, w, 4 * width * (m + w)),
        name="cross",
    )(at, s, *tiles)


def spread(x):
    h, w = x.shape
    sub = h // 24
    return lax.all_to_all(x.reshape(3, 8, sub, w), ROW, 1, 0, tiled=True).reshape(NB, sub, w)


def pick_rows_kernel(anc, x, out):
    for i in range(NANC):
        out[i] = x[anc[i]]


def pick_rows(ancestors, x):
    sub, w = x.shape[1:]
    return pl.pallas_call(
        pick_rows_kernel,
        out_shape=jax.ShapeDtypeStruct((NANC, sub, w), F32),
        in_specs=[SMEM, VMEM],
        out_specs=VMEM,
        compiler_params=params(8),
        name="pick_rows",
    )(ancestors, x).reshape(NANC * sub, w)


def pick_cols_kernel(anc, x, out):
    for i in range(NANC):
        for k in range(2):
            t = 2 * anc[i] + k
            off = pl.multiple_of(lax.rem(t, 3) * 128, 128)
            out[:, pl.ds(i * 256 + k * 128, 128)] = x[lax.div(t, 3), :, pl.ds(off, 128)]


def pick_cols(ancestors, x):
    return pl.pallas_call(
        pick_cols_kernel,
        out_shape=jax.ShapeDtypeStruct((x.shape[1], NANC * 256), F32),
        in_specs=[SMEM, VMEM],
        out_specs=VMEM,
        compiler_params=params(8),
        name="pick_cols",
    )(ancestors, x)


def per_device(sigma_top, factor_cross, factor_inverse, block_inverse, ancestors):
    h, w = sigma_top.shape
    sub = h // 24
    at, at_turned = places(False), places(True)

    f = pick_rows(ancestors, spread(factor_cross))
    inverse = lax.all_gather(after(factor_inverse, f), ROW, axis=0, tiled=True).reshape(16, w, w)
    f_near, f_far = gather_cols(f, True)

    s = pick_rows(ancestors, spread(after(sigma_top, f)))
    s = lax.all_to_all(after(s, f_near[0]).reshape(16, -1, w), COL, 0, 0, tiled=True)
    s_all = lax.all_gather(pick_cols(ancestors, s), COL, axis=0, tiled=True)

    (acc,) = near_product(at, f_near, inverse, 1, W1)
    u, ut = update_product(at, acc, *f_far, inverse)

    u_near, u_far = gather_cols(turn(ut), False)
    u_tiles = gather_rows(u.reshape(NANC, sub, w))

    sigma = cross_product(at, after(s_all, u_near[0]), u_tiles)
    sigma_all = lax.all_gather(sigma, ROW, axis=0, tiled=True).reshape(8, w, w)
    acc, rows = near_product(at_turned, u_near, sigma_all, 2, W2, ancestors)
    sigma_child = child_product(at_turned, acc, *u_far, sigma_all, block_inverse)

    return (rows.reshape(h, w), sigma_child)


def solution(mesh):
    fine = Mesh(np.asarray(mesh.devices).reshape(4, 2, 4, 4), ALL)
    tile = P(ROW, COL)
    return jax.shard_map(
        per_device,
        mesh=fine,
        in_specs=(tile, tile, tile, tile, P()),
        out_specs=(tile, tile),
        check_vma=False,
    )
```

```python
import functools

import jax
import jax.numpy as jnp
import numpy as np
from jax import lax
from jax.experimental import pallas as pl
from jax.experimental.pallas import tpu as pltpu
from jax.sharding import Mesh, PartitionSpec as P

NB = 24
NANC = 12
W1, W2 = 12, 12
ROW = ("y", "core")
COL = ("z", "x")
ALL = ("y", "core", "z", "x")
VMEM = pl.BlockSpec(memory_space=pltpu.VMEM)
SMEM = pl.BlockSpec(memory_space=pltpu.SMEM)
ANY = pl.BlockSpec(memory_space=pl.ANY)
HBM = pl.BlockSpec(memory_space=pltpu.HBM)
F32 = jnp.float32


def params(mib):
    return pltpu.CompilerParams(vmem_limit_bytes=mib * 1024 * 1024)


def cost(m, k, n, in_bytes):
    return pl.CostEstimate(flops=6 * m * k * n, bytes_accessed=in_bytes, transcendentals=0)


def after(x, *others):
    return lax.optimization_barrier((x, *others))[0]


def step(x):
    return lax.ppermute(x, ROW, [(2 * i + c, 2 * ((i + 1 - 2 * c) % 4) + c) for i in range(4) for c in range(2)])


def swap(x):
    return lax.ppermute(x, "core", [(0, 1), (1, 0)])


def gather_rows(x):
    mine = [x]
    for _ in range(3):
        mine.append(step(mine[-1]))
    return mine + [swap(t) for t in mine]


def hop(x, along, by):
    pairs = []
    for core in range(2):
        for i in range(4):
            for j in range(4):
                to = (i, (j + by) % 4) if along == core else ((i + by) % 4, j)
                pairs.append((16 * core + 4 * i + j, 16 * core + 4 * to[0] + to[1]))
    return lax.ppermute(x, ("core",) + COL, pairs)


def gather_cols(x, whole):
    half = x.shape[0] // 2
    up, down = hop(x, 0, 1), hop(x, 0, -1)
    top, low = hop(up[:half], 0, 1), hop(down[half:], 0, -1)
    if whole:
        group = jnp.stack([x, up, down, jnp.concatenate([top, low])])
        up, down = hop(group, 1, 1), hop(group, 1, -1)
        return (group, up, down), (hop(up[:2], 1, 1), hop(down[2:], 1, -1))
    one, two = jnp.stack([x, up]), jnp.stack([down, jnp.concatenate([top, low])])
    one, two = lax.optimization_barrier((one, two))
    up_one, down_two = hop(one, 1, 1), hop(two, 1, -1)
    up_two, down_one = hop(two, 1, 1), hop(one, 1, -1)
    return (one, two, up_one, up_two, down_one, down_two), (hop(up_one, 1, 1), hop(down_two, 1, -1))


def turn(x):
    at = lambda y, core, z, x: ((2 * y + core) * 4 + z) * 4 + x
    every = [(y, core, z, x) for y in range(4) for core in range(2) for z in range(4) for x in range(4)]
    x = lax.ppermute(x, ALL, [(at(y, c, z, x), at(y, x // 2, (y + z) % 4, 2 * c + x % 2)) for y, c, z, x in every])
    return lax.ppermute(x, ALL, [(at(y, c, z, x), at((z - y) % 4, c, z, x)) for y, c, z, x in every])


def places(turned):
    y, core, z, x = (lax.axis_index(n) for n in ALL)
    s = 1 - 2 * core
    near = lambda i, k: lax.rem(i + k + 8, 4)
    rows = [2 * near(y, -s * k) + core for k in range(4)] + [2 * near(y, s * k) + 1 - core for k in range(4)]
    first, second = jnp.where(core == 0, x, z), jnp.where(core == 0, z, x)
    cols = []
    for k in (0, -1, 1, 2):
        for i in (0, -1, 1, 2):
            u, v = near(first, i), near(second, k)
            at_z, at_x = jnp.where(core == 0, v, u), jnp.where(core == 0, u, v)
            cols.append(4 * (lax.rem(at_z - y + 4, 4) if turned else at_z) + at_x)
    return jnp.stack(rows + cols).astype(jnp.int32)


def dot3(a, b):
    a_hi, b_hi = a.astype(jnp.bfloat16), b.astype(jnp.bfloat16)
    a_lo = (a - a_hi.astype(F32)).astype(jnp.bfloat16)
    b_lo = (b - b_hi.astype(F32)).astype(jnp.bfloat16)
    mul = lambda p, q: jnp.dot(p, q, preferred_element_type=F32)
    both = mul(a_hi, jnp.concatenate([b_hi, b_lo], axis=1))
    n = b.shape[1]
    return both[:, :n] + (both[:, n:] + mul(a_lo, b_hi))


def near_child_kernel(per, count, anc, first, at, *refs):
    tiles, rows, sem = refs[count], refs[count + 2], refs[-1]
    blocks, _, sub, _ = rows.shape
    copies, living = [], []
    for b in range(blocks):
        hits = [jnp.where(anc[i] == first[0] + b, 1, 0) for i in range(NANC)]
        index = sum(i * hit for i, hit in enumerate(hits))
        living.append(sum(hits))
        source = tiles.at[:, pl.ds(pl.multiple_of(index * sub, 8), sub)]
        copies.append(pltpu.make_async_copy(source, rows.at[b], sem.at[b]))
    near_kernel(per, count, at, *refs[: count + 2], *refs[count + 3 : -1], others=copies)
    for b in range(blocks):
        copies[b].wait()

        @pl.when(living[b] == 0)
        def _():
            rows[b] = jnp.zeros_like(rows[b])


def near_kernel(per, count, at, *refs, others=()):
    pieces, tiles, acc, (a_buf, b_buf, a_sem, b_sem) = refs[:count], refs[count], refs[count + 1], refs[count + 2 :]
    outs, many = acc.shape[0], 12 // count

    def piece_copy(i, source):
        return pltpu.make_async_copy(source, a_buf.at[pl.ds(many * i, many)], a_sem.at[i])

    def tile_copy(k):
        return pltpu.make_async_copy(tiles.at[lax.div(at[8 + k], per)], b_buf.at[k], b_sem.at[k])

    for i in range(count):
        piece_copy(i, pieces[i]).start()
        for k in range(many):
            tile_copy(many * i + k).start()
    for copy in others:
        copy.start()
    acc[...] = jnp.zeros_like(acc)

    def body(i, carry):
        g, q = lax.div(i, 2), lax.rem(i, 2)

        @pl.when(q == 0)
        def _():
            for k in range(count // 3):
                piece_copy((count // 3) * g + k, pieces[0]).wait()

        k0, k1 = 4 * g + q, 4 * g + 3 - q
        tile_copy(k0).wait()
        tile_copy(k1).wait()
        acc[lax.rem(at[8 + k0], outs)] += dot3(
            jnp.concatenate([a_buf[k0], a_buf[k1]], axis=1), jnp.concatenate([b_buf[k0], b_buf[k1]], axis=0)
        )
        return carry

    lax.fori_loop(0, 6, body, 0)


def near_product(at, pieces, tiles, outs, weight, ancestors=None):
    m, w = pieces[0].shape[1:]
    many, _, n = tiles.shape
    kernel, extra, out_shape, more = near_kernel, (), [jax.ShapeDtypeStruct((outs, m, n), F32)], []
    if ancestors is not None:
        kernel, extra = near_child_kernel, (ancestors, (3 * lax.axis_index(ROW)).astype(jnp.int32).reshape(1))
        out_shape += [jax.ShapeDtypeStruct((3, many, m // NANC, n), F32)]
        more = [pltpu.SemaphoreType.DMA((3,))]
    return pl.pallas_call(
        functools.partial(kernel, 16 // many, len(pieces)),
        out_shape=out_shape,
        in_specs=[SMEM] * (1 + len(extra)) + [ANY] * len(pieces) + [HBM],
        out_specs=[VMEM] * len(out_shape),
        scratch_shapes=[
            pltpu.VMEM((12, m, w), F32),
            pltpu.VMEM((12,) + tiles.shape[1:], F32),
            pltpu.SemaphoreType.DMA((len(pieces),)),
            pltpu.SemaphoreType.DMA((12,)),
        ] + more,
        compiler_params=params(40),
        cost_estimate=cost(weight * m, 12 * w, n, weight * 4 * w * (12 * m + many * n)),
        name="near",
    )(*extra, at, *pieces, tiles)


def far_sum(at, top, low, tiles, a_buf, b_buf, sem, per):
    copies = [pltpu.make_async_copy(top, a_buf.at[pl.ds(0, 2)], sem.at[0])]
    copies += [pltpu.make_async_copy(low, a_buf.at[pl.ds(2, 2)], sem.at[1])]
    copies += [pltpu.make_async_copy(tiles.at[lax.div(at[20 + k], per)], b_buf.at[k], sem.at[2 + k]) for k in range(4)]
    for copy in copies:
        copy.start()
    for copy in copies:
        copy.wait()
    for q in range(2):
        yield q, dot3(
            jnp.concatenate([a_buf[q], a_buf[3 - q]], axis=1), jnp.concatenate([b_buf[q], b_buf[3 - q]], axis=0)
        )


def far_scratch(top, tiles):
    return [
        pltpu.VMEM((4,) + top.shape[1:], F32),
        pltpu.VMEM((4,) + tiles.shape[1:], F32),
        pltpu.SemaphoreType.DMA((6,)),
    ]


def update_kernel(at, acc, top, low, tiles, u, ut, a_buf, b_buf, sem):
    total = acc[0]
    for _, part in far_sum(at, top, low, tiles, a_buf, b_buf, sem, 1):
        total += part
    u[...] = total
    ut[...] = total.T


def update_product(at, acc, top, low, tiles):
    _, m, n = acc.shape
    return pl.pallas_call(
        update_kernel,
        out_shape=(jax.ShapeDtypeStruct((m, n), F32), jax.ShapeDtypeStruct((n, m), F32)),
        in_specs=[SMEM, VMEM, ANY, ANY, HBM],
        out_specs=(VMEM, VMEM),
        scratch_shapes=far_scratch(top, tiles),
        compiler_params=params(24),
        cost_estimate=cost(m, 4 * top.shape[2], n, 16 * m * n),
        name="update",
    )(at, acc, top, low, tiles)


def child_kernel(at, acc, top, low, tiles, base, child, a_buf, b_buf, sem):
    w = acc.shape[1]
    for p in range(2):
        child[pl.ds(p * w, w)] = base[pl.ds(p * w, w)] - acc[p]
    for q, part in far_sum(at, top, low, tiles, a_buf, b_buf, sem, 2):
        p = pl.multiple_of(lax.rem(at[20 + q], 2) * w, 8)
        child[pl.ds(p, w)] -= part


def child_product(at, acc, top, low, tiles, base):
    return pl.pallas_call(
        child_kernel,
        out_shape=jax.ShapeDtypeStruct(base.shape, F32),
        in_specs=[SMEM, VMEM, ANY, ANY, HBM, VMEM],
        out_specs=VMEM,
        scratch_shapes=far_scratch(top, tiles),
        compiler_params=params(24),
        cost_estimate=cost(acc.shape[1], 4 * top.shape[2], acc.shape[2], 24 * acc.shape[1] * acc.shape[2]),
        name="child",
    )(at, acc, top, low, tiles, base)


def cross_kernel(at, s, *refs):
    tiles, (sigma, s_buf, u_buf, s_sem, u_sem) = refs[:8], refs[8:]
    m, w = sigma.shape

    def s_copy(k):
        return pltpu.make_async_copy(s.at[:, pl.ds(768 * k, 768)], s_buf.at[k], s_sem.at[k])

    copies = [pltpu.make_async_copy(tiles[i], u_buf.at[:, at[i]], u_sem.at[i]) for i in range(8)]
    for copy in copies:
        copy.start()
    for k in range(4):
        s_copy(k).start()
    sigma[...] = jnp.zeros_like(sigma)
    for copy in copies:
        copy.wait()
    for k in range(4):
        s_copy(k).wait()
        sigma[...] -= dot3(s_buf[k], u_buf[pl.ds(3 * k, 3)].reshape(768, w))


def cross_product(at, s, tiles):
    m, width = s.shape
    sub, w = tiles[0].shape[1:]
    return pl.pallas_call(
        cross_kernel,
        out_shape=jax.ShapeDtypeStruct((m, w), F32),
        in_specs=[SMEM, HBM] + [ANY] * 8,
        out_specs=VMEM,
        scratch_shapes=[
            pltpu.VMEM((4, m, 768), F32),
            pltpu.VMEM((NANC, 8, sub, w), F32),
            pltpu.SemaphoreType.DMA((4,)),
            pltpu.SemaphoreType.DMA((8,)),
        ],
        compiler_params=params(40),
        cost_estimate=cost(m, width, w, 4 * width * (m + w)),
        name="cross",
    )(at, s, *tiles)


def spread(x):
    h, w = x.shape
    sub = h // 24
    return lax.all_to_all(x.reshape(3, 8, sub, w), ROW, 1, 0, tiled=True).reshape(NB, sub, w)


def pick_rows_kernel(anc, x, out):
    for i in range(NANC):
        out[i] = x[anc[i]]


def pick_rows(ancestors, x):
    sub, w = x.shape[1:]
    return pl.pallas_call(
        pick_rows_kernel,
        out_shape=jax.ShapeDtypeStruct((NANC, sub, w), F32),
        in_specs=[SMEM, VMEM],
        out_specs=VMEM,
        compiler_params=params(8),
        name="pick_rows",
    )(ancestors, x).reshape(NANC * sub, w)


def pick_cols_kernel(anc, x, out):
    for i in range(NANC):
        for k in range(2):
            t = 2 * anc[i] + k
            off = pl.multiple_of(lax.rem(t, 3) * 128, 128)
            out[:, pl.ds(i * 256 + k * 128, 128)] = x[lax.div(t, 3), :, pl.ds(off, 128)]


def pick_cols(ancestors, x):
    return pl.pallas_call(
        pick_cols_kernel,
        out_shape=jax.ShapeDtypeStruct((x.shape[1], NANC * 256), F32),
        in_specs=[SMEM, VMEM],
        out_specs=VMEM,
        compiler_params=params(8),
        name="pick_cols",
    )(ancestors, x)


def per_device(sigma_top, factor_cross, factor_inverse, block_inverse, ancestors):
    h, w = sigma_top.shape
    sub = h // 24
    at, at_turned = places(False), places(True)

    f = pick_rows(ancestors, spread(factor_cross))
    inverse = lax.all_gather(after(factor_inverse, f), ROW, axis=0, tiled=True).reshape(16, w, w)
    f_near, f_far = gather_cols(f, True)

    s = pick_rows(ancestors, spread(after(sigma_top, f)))
    s = lax.all_to_all(after(s, f_near[0]).reshape(16, -1, w), COL, 0, 0, tiled=True)
    s_all = lax.all_gather(pick_cols(ancestors, s), COL, axis=0, tiled=True)

    (acc,) = near_product(at, f_near, inverse, 1, W1)
    u, ut = update_product(at, acc, *f_far, inverse)

    u_near, u_far = gather_cols(turn(ut), False)
    u_tiles = gather_rows(u.reshape(NANC, sub, w))

    sigma = cross_product(at, after(s_all, u_near[0]), u_tiles)
    sigma_all = lax.all_gather(sigma, ROW, axis=0, tiled=True).reshape(8, w, w)
    acc, rows = near_product(at_turned, u_near, sigma_all, 2, W2, ancestors)
    sigma_child = child_product(at_turned, acc, *u_far, sigma_all, block_inverse)

    return (rows.reshape(h, w), sigma_child)


def solution(mesh):
    fine = Mesh(np.asarray(mesh.devices).reshape(4, 2, 4, 4), ALL)
    tile = P(ROW, COL)
    return jax.shard_map(
        per_device,
        mesh=fine,
        in_specs=(tile, tile, tile, tile, P()),
        out_specs=(tile, tile),
        check_vma=False,
    )
```

```python
import functools

import jax
import jax.numpy as jnp
import numpy as np
from jax import lax
from jax.experimental import pallas as pl
from jax.experimental.pallas import tpu as pltpu
from jax.sharding import Mesh, PartitionSpec as P

NB = 24
NANC = 12
W1, W2 = 12, 12
ROW = ("y", "core")
COL = ("z", "x")
ALL = ("y", "core", "z", "x")
VMEM = pl.BlockSpec(memory_space=pltpu.VMEM)
SMEM = pl.BlockSpec(memory_space=pltpu.SMEM)
ANY = pl.BlockSpec(memory_space=pl.ANY)
HBM = pl.BlockSpec(memory_space=pltpu.HBM)
F32 = jnp.float32


def params(mib):
    return pltpu.CompilerParams(vmem_limit_bytes=mib * 1024 * 1024)


def cost(m, k, n, in_bytes):
    return pl.CostEstimate(flops=6 * m * k * n, bytes_accessed=in_bytes, transcendentals=0)


def after(x, *others):
    return lax.optimization_barrier((x, *others))[0]


def step(x):
    return lax.ppermute(x, ROW, [(2 * i + c, 2 * ((i + 1 - 2 * c) % 4) + c) for i in range(4) for c in range(2)])


def swap(x):
    return lax.ppermute(x, "core", [(0, 1), (1, 0)])


def gather_rows(x):
    mine = [x]
    for _ in range(3):
        mine.append(step(mine[-1]))
    return mine + [swap(t) for t in mine]


def hop(x, along, by):
    pairs = []
    for core in range(2):
        for i in range(4):
            for j in range(4):
                to = (i, (j + by) % 4) if along == core else ((i + by) % 4, j)
                pairs.append((16 * core + 4 * i + j, 16 * core + 4 * to[0] + to[1]))
    return lax.ppermute(x, ("core",) + COL, pairs)


def gather_cols(x, whole):
    half = x.shape[0] // 2
    up, down = hop(x, 0, 1), hop(x, 0, -1)
    top, low = hop(up[:half], 0, 1), hop(down[half:], 0, -1)
    if whole:
        group = jnp.stack([x, up, down, jnp.concatenate([top, low])])
        up, down = hop(group, 1, 1), hop(group, 1, -1)
        return (group, up, down), (hop(up[:2], 1, 1), hop(down[2:], 1, -1)), top
    one, two = jnp.stack([x, up]), jnp.stack([down, jnp.concatenate([top, low])])
    one, two = lax.optimization_barrier((one, two))
    up_one, down_two = hop(one, 1, 1), hop(two, 1, -1)
    up_two, down_one = hop(two, 1, 1), hop(one, 1, -1)
    return (one, two, up_one, up_two, down_one, down_two), (hop(up_one, 1, 1), hop(down_two, 1, -1)), top


def turn(x):
    at = lambda y, core, z, x: ((2 * y + core) * 4 + z) * 4 + x
    every = [(y, core, z, x) for y in range(4) for core in range(2) for z in range(4) for x in range(4)]
    x = lax.ppermute(x, ALL, [(at(y, c, z, x), at(y, x // 2, (y + z) % 4, 2 * c + x % 2)) for y, c, z, x in every])
    return lax.ppermute(x, ALL, [(at(y, c, z, x), at((z - y) % 4, c, z, x)) for y, c, z, x in every])


def places(turned):
    y, core, z, x = (lax.axis_index(n) for n in ALL)
    s = 1 - 2 * core
    near = lambda i, k: lax.rem(i + k + 8, 4)
    rows = [2 * near(y, -s * k) + core for k in range(4)] + [2 * near(y, s * k) + 1 - core for k in range(4)]
    first, second = jnp.where(core == 0, x, z), jnp.where(core == 0, z, x)
    cols = []
    for k in (0, -1, 1, 2):
        for i in (0, -1, 1, 2):
            u, v = near(first, i), near(second, k)
            at_z, at_x = jnp.where(core == 0, v, u), jnp.where(core == 0, u, v)
            cols.append(4 * (lax.rem(at_z - y + 4, 4) if turned else at_z) + at_x)
    return jnp.stack(rows + cols).astype(jnp.int32)


def dot3(a, b):
    a_hi, b_hi = a.astype(jnp.bfloat16), b.astype(jnp.bfloat16)
    a_lo = (a - a_hi.astype(F32)).astype(jnp.bfloat16)
    b_lo = (b - b_hi.astype(F32)).astype(jnp.bfloat16)
    mul = lambda p, q: jnp.dot(p, q, preferred_element_type=F32)
    both = mul(a_hi, jnp.concatenate([b_hi, b_lo], axis=1))
    n = b.shape[1]
    return both[:, :n] + (both[:, n:] + mul(a_lo, b_hi))


def near_child_kernel(per, count, anc, first, at, *refs):
    tiles, rows, sem = refs[count], refs[count + 2], refs[-1]
    blocks, _, sub, _ = rows.shape
    copies, living = [], []
    for b in range(blocks):
        hits = [jnp.where(anc[i] == first[0] + b, 1, 0) for i in range(NANC)]
        index = sum(i * hit for i, hit in enumerate(hits))
        living.append(sum(hits))
        source = tiles.at[:, pl.ds(pl.multiple_of(index * sub, 8), sub)]
        copies.append(pltpu.make_async_copy(source, rows.at[b], sem.at[b]))
    near_kernel(per, count, at, *refs[: count + 2], *refs[count + 3 : -1], others=copies)
    for b in range(blocks):
        copies[b].wait()

        @pl.when(living[b] == 0)
        def _():
            rows[b] = jnp.zeros_like(rows[b])


def near_kernel(per, count, at, *refs, others=()):
    pieces, tiles, acc, (a_buf, b_buf, a_sem, b_sem) = refs[:count], refs[count], refs[count + 1], refs[count + 2 :]
    outs, many = acc.shape[0], 12 // count

    def piece_copy(i, source):
        return pltpu.make_async_copy(source, a_buf.at[pl.ds(many * i, many)], a_sem.at[i])

    def tile_copy(k):
        return pltpu.make_async_copy(tiles.at[lax.div(at[8 + k], per)], b_buf.at[k], b_sem.at[k])

    for i in range(count):
        piece_copy(i, pieces[i]).start()
        for k in range(many):
            tile_copy(many * i + k).start()
    for copy in others:
        copy.start()
    acc[...] = jnp.zeros_like(acc)

    def body(i, carry):
        g, q = lax.div(i, 2), lax.rem(i, 2)

        @pl.when(q == 0)
        def _():
            for k in range(count // 3):
                piece_copy((count // 3) * g + k, pieces[0]).wait()

        k0, k1 = 4 * g + q, 4 * g + 3 - q
        tile_copy(k0).wait()
        tile_copy(k1).wait()
        acc[lax.rem(at[8 + k0], outs)] += dot3(
            jnp.concatenate([a_buf[k0], a_buf[k1]], axis=1), jnp.concatenate([b_buf[k0], b_buf[k1]], axis=0)
        )
        return carry

    lax.fori_loop(0, 6, body, 0)


def near_product(at, pieces, tiles, outs, weight, ancestors=None):
    m, w = pieces[0].shape[1:]
    many, _, n = tiles.shape
    kernel, extra, out_shape, more = near_kernel, (), [jax.ShapeDtypeStruct((outs, m, n), F32)], []
    if ancestors is not None:
        kernel, extra = near_child_kernel, (ancestors, (3 * lax.axis_index(ROW)).astype(jnp.int32).reshape(1))
        out_shape += [jax.ShapeDtypeStruct((3, many, m // NANC, n), F32)]
        more = [pltpu.SemaphoreType.DMA((3,))]
    return pl.pallas_call(
        functools.partial(kernel, 16 // many, len(pieces)),
        out_shape=out_shape,
        in_specs=[SMEM] * (1 + len(extra)) + [ANY] * len(pieces) + [HBM],
        out_specs=[VMEM] * len(out_shape),
        scratch_shapes=[
            pltpu.VMEM((12, m, w), F32),
            pltpu.VMEM((12,) + tiles.shape[1:], F32),
            pltpu.SemaphoreType.DMA((len(pieces),)),
            pltpu.SemaphoreType.DMA((12,)),
        ] + more,
        compiler_params=params(40),
        cost_estimate=cost(weight * m, 12 * w, n, weight * 4 * w * (12 * m + many * n)),
        name="near",
    )(*extra, at, *pieces, tiles)


def far_sum(at, top, low, tiles, a_buf, b_buf, sem, per):
    copies = [pltpu.make_async_copy(top, a_buf.at[pl.ds(0, 2)], sem.at[0])]
    copies += [pltpu.make_async_copy(low, a_buf.at[pl.ds(2, 2)], sem.at[1])]
    copies += [pltpu.make_async_copy(tiles.at[lax.div(at[20 + k], per)], b_buf.at[k], sem.at[2 + k]) for k in range(4)]
    for copy in copies:
        copy.start()
    for copy in copies:
        copy.wait()
    for q in range(2):
        yield q, dot3(
            jnp.concatenate([a_buf[q], a_buf[3 - q]], axis=1), jnp.concatenate([b_buf[q], b_buf[3 - q]], axis=0)
        )


def far_scratch(top, tiles):
    return [
        pltpu.VMEM((4,) + top.shape[1:], F32),
        pltpu.VMEM((4,) + tiles.shape[1:], F32),
        pltpu.SemaphoreType.DMA((6,)),
    ]


def update_kernel(at, acc, top, low, tiles, u, ut, a_buf, b_buf, sem):
    total = acc[0]
    for _, part in far_sum(at, top, low, tiles, a_buf, b_buf, sem, 1):
        total += part
    u[...] = total
    ut[...] = total.T


def update_product(at, acc, top, low, tiles):
    _, m, n = acc.shape
    return pl.pallas_call(
        update_kernel,
        out_shape=(jax.ShapeDtypeStruct((m, n), F32), jax.ShapeDtypeStruct((n, m), F32)),
        in_specs=[SMEM, VMEM, ANY, ANY, HBM],
        out_specs=(VMEM, VMEM),
        scratch_shapes=far_scratch(top, tiles),
        compiler_params=params(24),
        cost_estimate=cost(m, 4 * top.shape[2], n, 16 * m * n),
        name="update",
    )(at, acc, top, low, tiles)


def child_kernel(at, acc, top, low, tiles, base, child, a_buf, b_buf, sem):
    w = acc.shape[1]
    for p in range(2):
        child[pl.ds(p * w, w)] = base[pl.ds(p * w, w)] - acc[p]
    for q, part in far_sum(at, top, low, tiles, a_buf, b_buf, sem, 2):
        p = pl.multiple_of(lax.rem(at[20 + q], 2) * w, 8)
        child[pl.ds(p, w)] -= part


def child_product(at, acc, top, low, tiles, base):
    return pl.pallas_call(
        child_kernel,
        out_shape=jax.ShapeDtypeStruct(base.shape, F32),
        in_specs=[SMEM, VMEM, ANY, ANY, HBM, VMEM],
        out_specs=VMEM,
        scratch_shapes=far_scratch(top, tiles),
        compiler_params=params(24),
        cost_estimate=cost(acc.shape[1], 4 * top.shape[2], acc.shape[2], 24 * acc.shape[1] * acc.shape[2]),
        name="child",
    )(at, acc, top, low, tiles, base)


def cross_kernel(at, s, *refs):
    tiles, (sigma, s_buf, u_buf, s_sem, u_sem) = refs[:8], refs[8:]
    m, w = sigma.shape

    def s_copy(k):
        return pltpu.make_async_copy(s.at[:, pl.ds(768 * k, 768)], s_buf.at[k], s_sem.at[k])

    copies = [pltpu.make_async_copy(tiles[i], u_buf.at[:, at[i]], u_sem.at[i]) for i in range(8)]
    for copy in copies:
        copy.start()
    for k in range(4):
        s_copy(k).start()
    sigma[...] = jnp.zeros_like(sigma)
    for copy in copies:
        copy.wait()
    for k in range(4):
        s_copy(k).wait()
        sigma[...] -= dot3(s_buf[k], u_buf[pl.ds(3 * k, 3)].reshape(768, w))


def cross_product(at, s, tiles):
    m, width = s.shape
    sub, w = tiles[0].shape[1:]
    return pl.pallas_call(
        cross_kernel,
        out_shape=jax.ShapeDtypeStruct((m, w), F32),
        in_specs=[SMEM, HBM] + [ANY] * 8,
        out_specs=VMEM,
        scratch_shapes=[
            pltpu.VMEM((4, m, 768), F32),
            pltpu.VMEM((NANC, 8, sub, w), F32),
            pltpu.SemaphoreType.DMA((4,)),
            pltpu.SemaphoreType.DMA((8,)),
        ],
        compiler_params=params(40),
        cost_estimate=cost(m, width, w, 4 * width * (m + w)),
        name="cross",
    )(at, s, *tiles)


def spread(x):
    h, w = x.shape
    sub = h // 24
    return lax.all_to_all(x.reshape(3, 8, sub, w), ROW, 1, 0, tiled=True).reshape(NB, sub, w)


def pick_rows_kernel(anc, x, out):
    for i in range(NANC):
        out[i] = x[anc[i]]


def pick_rows(ancestors, x):
    sub, w = x.shape[1:]
    return pl.pallas_call(
        pick_rows_kernel,
        out_shape=jax.ShapeDtypeStruct((NANC, sub, w), F32),
        in_specs=[SMEM, VMEM],
        out_specs=VMEM,
        compiler_params=params(8),
        name="pick_rows",
    )(ancestors, x).reshape(NANC * sub, w)


def pick_cols_kernel(anc, x, out):
    for i in range(NANC):
        for k in range(2):
            t = 2 * anc[i] + k
            off = pl.multiple_of(lax.rem(t, 3) * 128, 128)
            out[:, pl.ds(i * 256 + k * 128, 128)] = x[lax.div(t, 3), :, pl.ds(off, 128)]


def pick_cols(ancestors, x):
    return pl.pallas_call(
        pick_cols_kernel,
        out_shape=jax.ShapeDtypeStruct((x.shape[1], NANC * 256), F32),
        in_specs=[SMEM, VMEM],
        out_specs=VMEM,
        compiler_params=params(8),
        name="pick_cols",
    )(ancestors, x)


def per_device(sigma_top, factor_cross, factor_inverse, block_inverse, ancestors):
    h, w = sigma_top.shape
    sub = h // 24
    at, at_turned = places(False), places(True)

    f = pick_rows(ancestors, spread(factor_cross))
    inverse = lax.all_gather(after(factor_inverse, f), ROW, axis=0, tiled=True).reshape(16, w, w)
    f_near, f_far, _ = gather_cols(f, True)

    s = pick_rows(ancestors, spread(after(sigma_top, f)))
    s = lax.all_to_all(after(s, f_near[0]).reshape(16, -1, w), COL, 0, 0, tiled=True)
    s_all = lax.all_gather(pick_cols(ancestors, s), COL, axis=0, tiled=True)

    (acc,) = near_product(at, f_near, inverse, 1, W1)
    u, ut = update_product(at, acc, *f_far, inverse)

    u_near, u_far, u_top = gather_cols(turn(ut), False)
    u_tiles = gather_rows(u.reshape(NANC, sub, w))

    sigma = cross_product(at, after(s_all, u_top), u_tiles)
    sigma_all = lax.all_gather(sigma, ROW, axis=0, tiled=True).reshape(8, w, w)
    acc, rows = near_product(at_turned, u_near, sigma_all, 2, W2, ancestors)
    sigma_child = child_product(at_turned, acc, *u_far, sigma_all, block_inverse)

    return (rows.reshape(h, w), sigma_child)


def solution(mesh):
    fine = Mesh(np.asarray(mesh.devices).reshape(4, 2, 4, 4), ALL)
    tile = P(ROW, COL)
    return jax.shard_map(
        per_device,
        mesh=fine,
        in_specs=(tile, tile, tile, tile, P()),
        out_specs=(tile, tile),
        check_vma=False,
    )
```

```python
import functools

import jax
import jax.numpy as jnp
import numpy as np
from jax import lax
from jax.experimental import pallas as pl
from jax.experimental.pallas import tpu as pltpu
from jax.sharding import Mesh, PartitionSpec as P

NB = 24
NANC = 12
W1, W2 = 12, 12
ROW = ("y", "core")
COL = ("z", "x")
ALL = ("y", "core", "z", "x")
VMEM = pl.BlockSpec(memory_space=pltpu.VMEM)
SMEM = pl.BlockSpec(memory_space=pltpu.SMEM)
ANY = pl.BlockSpec(memory_space=pl.ANY)
HBM = pl.BlockSpec(memory_space=pltpu.HBM)
F32 = jnp.float32


def params(mib):
    return pltpu.CompilerParams(vmem_limit_bytes=mib * 1024 * 1024)


def cost(m, k, n, in_bytes):
    return pl.CostEstimate(flops=6 * m * k * n, bytes_accessed=in_bytes, transcendentals=0)


def after(x, *others):
    return lax.optimization_barrier((x, *others))[0]


def step(x):
    return lax.ppermute(x, ROW, [(2 * i + c, 2 * ((i + 1 - 2 * c) % 4) + c) for i in range(4) for c in range(2)])


def swap(x):
    return lax.ppermute(x, "core", [(0, 1), (1, 0)])


def gather_rows(x):
    mine = [x]
    for _ in range(3):
        mine.append(step(mine[-1]))
    return mine + [swap(t) for t in mine]


def hop(x, along, by):
    pairs = []
    for core in range(2):
        for i in range(4):
            for j in range(4):
                to = (i, (j + by) % 4) if along == core else ((i + by) % 4, j)
                pairs.append((16 * core + 4 * i + j, 16 * core + 4 * to[0] + to[1]))
    return lax.ppermute(x, ("core",) + COL, pairs)


def gather_cols(x, whole):
    half = x.shape[0] // 2
    up, down = hop(x, 0, 1), hop(x, 0, -1)
    if not whole:
        up, down = lax.optimization_barrier((up, down))
    top, low = hop(up[:half], 0, 1), hop(down[half:], 0, -1)
    if whole:
        group = jnp.stack([x, up, down, jnp.concatenate([top, low])])
        up, down = hop(group, 1, 1), hop(group, 1, -1)
        return (group, up, down), (hop(up[:2], 1, 1), hop(down[2:], 1, -1)), top
    one, two = jnp.stack([x, up]), jnp.stack([down, jnp.concatenate([top, low])])
    one, two = lax.optimization_barrier((one, two))
    up_one, down_two = hop(one, 1, 1), hop(two, 1, -1)
    up_two, down_one = hop(two, 1, 1), hop(one, 1, -1)
    return (one, two, up_one, up_two, down_one, down_two), (hop(up_one, 1, 1), hop(down_two, 1, -1)), top


def turn(x):
    at = lambda y, core, z, x: ((2 * y + core) * 4 + z) * 4 + x
    every = [(y, core, z, x) for y in range(4) for core in range(2) for z in range(4) for x in range(4)]
    x = lax.ppermute(x, ALL, [(at(y, c, z, x), at(y, x // 2, (y + z) % 4, 2 * c + x % 2)) for y, c, z, x in every])
    return lax.ppermute(x, ALL, [(at(y, c, z, x), at((z - y) % 4, c, z, x)) for y, c, z, x in every])


def places(turned):
    y, core, z, x = (lax.axis_index(n) for n in ALL)
    s = 1 - 2 * core
    near = lambda i, k: lax.rem(i + k + 8, 4)
    rows = [2 * near(y, -s * k) + core for k in range(4)] + [2 * near(y, s * k) + 1 - core for k in range(4)]
    first, second = jnp.where(core == 0, x, z), jnp.where(core == 0, z, x)
    cols = []
    for k in (0, -1, 1, 2):
        for i in (0, -1, 1, 2):
            u, v = near(first, i), near(second, k)
            at_z, at_x = jnp.where(core == 0, v, u), jnp.where(core == 0, u, v)
            cols.append(4 * (lax.rem(at_z - y + 4, 4) if turned else at_z) + at_x)
    return jnp.stack(rows + cols).astype(jnp.int32)


def dot3(a, b):
    a_hi, b_hi = a.astype(jnp.bfloat16), b.astype(jnp.bfloat16)
    a_lo = (a - a_hi.astype(F32)).astype(jnp.bfloat16)
    b_lo = (b - b_hi.astype(F32)).astype(jnp.bfloat16)
    mul = lambda p, q: jnp.dot(p, q, preferred_element_type=F32)
    both = mul(a_hi, jnp.concatenate([b_hi, b_lo], axis=1))
    n = b.shape[1]
    return both[:, :n] + (both[:, n:] + mul(a_lo, b_hi))


def near_child_kernel(per, count, anc, first, at, *refs):
    tiles, rows, sem = refs[count], refs[count + 2], refs[-1]
    blocks, _, sub, _ = rows.shape
    copies, living = [], []
    for b in range(blocks):
        hits = [jnp.where(anc[i] == first[0] + b, 1, 0) for i in range(NANC)]
        index = sum(i * hit for i, hit in enumerate(hits))
        living.append(sum(hits))
        source = tiles.at[:, pl.ds(pl.multiple_of(index * sub, 8), sub)]
        copies.append(pltpu.make_async_copy(source, rows.at[b], sem.at[b]))
    near_kernel(per, count, at, *refs[: count + 2], *refs[count + 3 : -1], others=copies)
    for b in range(blocks):
        copies[b].wait()

        @pl.when(living[b] == 0)
        def _():
            rows[b] = jnp.zeros_like(rows[b])


def near_kernel(per, count, at, *refs, others=()):
    pieces, tiles, acc, (a_buf, b_buf, a_sem, b_sem) = refs[:count], refs[count], refs[count + 1], refs[count + 2 :]
    outs, many = acc.shape[0], 12 // count

    def piece_copy(i, source):
        return pltpu.make_async_copy(source, a_buf.at[pl.ds(many * i, many)], a_sem.at[i])

    def tile_copy(k):
        return pltpu.make_async_copy(tiles.at[lax.div(at[8 + k], per)], b_buf.at[k], b_sem.at[k])

    for i in range(count):
        piece_copy(i, pieces[i]).start()
        for k in range(many):
            tile_copy(many * i + k).start()
    for copy in others:
        copy.start()
    acc[...] = jnp.zeros_like(acc)

    def body(i, carry):
        g, q = lax.div(i, 2), lax.rem(i, 2)

        @pl.when(q == 0)
        def _():
            for k in range(count // 3):
                piece_copy((count // 3) * g + k, pieces[0]).wait()

        k0, k1 = 4 * g + q, 4 * g + 3 - q
        tile_copy(k0).wait()
        tile_copy(k1).wait()
        acc[lax.rem(at[8 + k0], outs)] += dot3(
            jnp.concatenate([a_buf[k0], a_buf[k1]], axis=1), jnp.concatenate([b_buf[k0], b_buf[k1]], axis=0)
        )
        return carry

    lax.fori_loop(0, 6, body, 0)


def near_product(at, pieces, tiles, outs, weight, ancestors=None):
    m, w = pieces[0].shape[1:]
    many, _, n = tiles.shape
    kernel, extra, out_shape, more = near_kernel, (), [jax.ShapeDtypeStruct((outs, m, n), F32)], []
    if ancestors is not None:
        kernel, extra = near_child_kernel, (ancestors, (3 * lax.axis_index(ROW)).astype(jnp.int32).reshape(1))
        out_shape += [jax.ShapeDtypeStruct((3, many, m // NANC, n), F32)]
        more = [pltpu.SemaphoreType.DMA((3,))]
    return pl.pallas_call(
        functools.partial(kernel, 16 // many, len(pieces)),
        out_shape=out_shape,
        in_specs=[SMEM] * (1 + len(extra)) + [ANY] * len(pieces) + [HBM],
        out_specs=[VMEM] * len(out_shape),
        scratch_shapes=[
            pltpu.VMEM((12, m, w), F32),
            pltpu.VMEM((12,) + tiles.shape[1:], F32),
            pltpu.SemaphoreType.DMA((len(pieces),)),
            pltpu.SemaphoreType.DMA((12,)),
        ] + more,
        compiler_params=params(40),
        cost_estimate=cost(weight * m, 12 * w, n, weight * 4 * w * (12 * m + many * n)),
        name="near",
    )(*extra, at, *pieces, tiles)


def far_sum(at, top, low, tiles, a_buf, b_buf, sem, per):
    copies = [pltpu.make_async_copy(top, a_buf.at[pl.ds(0, 2)], sem.at[0])]
    copies += [pltpu.make_async_copy(low, a_buf.at[pl.ds(2, 2)], sem.at[1])]
    copies += [pltpu.make_async_copy(tiles.at[lax.div(at[20 + k], per)], b_buf.at[k], sem.at[2 + k]) for k in range(4)]
    for copy in copies:
        copy.start()
    for copy in copies:
        copy.wait()
    for q in range(2):
        yield q, dot3(
            jnp.concatenate([a_buf[q], a_buf[3 - q]], axis=1), jnp.concatenate([b_buf[q], b_buf[3 - q]], axis=0)
        )


def far_scratch(top, tiles):
    return [
        pltpu.VMEM((4,) + top.shape[1:], F32),
        pltpu.VMEM((4,) + tiles.shape[1:], F32),
        pltpu.SemaphoreType.DMA((6,)),
    ]


def update_kernel(at, acc, top, low, tiles, u, ut, a_buf, b_buf, sem):
    total = acc[0]
    for _, part in far_sum(at, top, low, tiles, a_buf, b_buf, sem, 1):
        total += part
    u[...] = total
    ut[...] = total.T


def update_product(at, acc, top, low, tiles):
    _, m, n = acc.shape
    return pl.pallas_call(
        update_kernel,
        out_shape=(jax.ShapeDtypeStruct((m, n), F32), jax.ShapeDtypeStruct((n, m), F32)),
        in_specs=[SMEM, VMEM, ANY, ANY, HBM],
        out_specs=(VMEM, VMEM),
        scratch_shapes=far_scratch(top, tiles),
        compiler_params=params(24),
        cost_estimate=cost(m, 4 * top.shape[2], n, 16 * m * n),
        name="update",
    )(at, acc, top, low, tiles)


def child_kernel(at, acc, top, low, tiles, base, child, a_buf, b_buf, sem):
    w = acc.shape[1]
    for p in range(2):
        child[pl.ds(p * w, w)] = base[pl.ds(p * w, w)] - acc[p]
    for q, part in far_sum(at, top, low, tiles, a_buf, b_buf, sem, 2):
        p = pl.multiple_of(lax.rem(at[20 + q], 2) * w, 8)
        child[pl.ds(p, w)] -= part


def child_product(at, acc, top, low, tiles, base):
    return pl.pallas_call(
        child_kernel,
        out_shape=jax.ShapeDtypeStruct(base.shape, F32),
        in_specs=[SMEM, VMEM, ANY, ANY, HBM, VMEM],
        out_specs=VMEM,
        scratch_shapes=far_scratch(top, tiles),
        compiler_params=params(24),
        cost_estimate=cost(acc.shape[1], 4 * top.shape[2], acc.shape[2], 24 * acc.shape[1] * acc.shape[2]),
        name="child",
    )(at, acc, top, low, tiles, base)


def cross_kernel(at, s, *refs):
    tiles, (sigma, s_buf, u_buf, s_sem, u_sem) = refs[:8], refs[8:]
    m, w = sigma.shape

    def s_copy(k):
        return pltpu.make_async_copy(s.at[:, pl.ds(768 * k, 768)], s_buf.at[k], s_sem.at[k])

    copies = [pltpu.make_async_copy(tiles[i], u_buf.at[:, at[i]], u_sem.at[i]) for i in range(8)]
    for copy in copies:
        copy.start()
    for k in range(4):
        s_copy(k).start()
    sigma[...] = jnp.zeros_like(sigma)
    for copy in copies:
        copy.wait()
    for k in range(4):
        s_copy(k).wait()
        sigma[...] -= dot3(s_buf[k], u_buf[pl.ds(3 * k, 3)].reshape(768, w))


def cross_product(at, s, tiles):
    m, width = s.shape
    sub, w = tiles[0].shape[1:]
    return pl.pallas_call(
        cross_kernel,
        out_shape=jax.ShapeDtypeStruct((m, w), F32),
        in_specs=[SMEM, HBM] + [ANY] * 8,
        out_specs=VMEM,
        scratch_shapes=[
            pltpu.VMEM((4, m, 768), F32),
            pltpu.VMEM((NANC, 8, sub, w), F32),
            pltpu.SemaphoreType.DMA((4,)),
            pltpu.SemaphoreType.DMA((8,)),
        ],
        compiler_params=params(40),
        cost_estimate=cost(m, width, w, 4 * width * (m + w)),
        name="cross",
    )(at, s, *tiles)


def spread(x):
    h, w = x.shape
    sub = h // 24
    return lax.all_to_all(x.reshape(3, 8, sub, w), ROW, 1, 0, tiled=True).reshape(NB, sub, w)


def pick_rows_kernel(anc, x, out):
    for i in range(NANC):
        out[i] = x[anc[i]]


def pick_rows(ancestors, x):
    sub, w = x.shape[1:]
    return pl.pallas_call(
        pick_rows_kernel,
        out_shape=jax.ShapeDtypeStruct((NANC, sub, w), F32),
        in_specs=[SMEM, VMEM],
        out_specs=VMEM,
        compiler_params=params(8),
        name="pick_rows",
    )(ancestors, x).reshape(NANC * sub, w)


def pick_cols_kernel(anc, x, out):
    for i in range(NANC):
        for k in range(2):
            t = 2 * anc[i] + k
            off = pl.multiple_of(lax.rem(t, 3) * 128, 128)
            out[:, pl.ds(i * 256 + k * 128, 128)] = x[lax.div(t, 3), :, pl.ds(off, 128)]


def pick_cols(ancestors, x):
    return pl.pallas_call(
        pick_cols_kernel,
        out_shape=jax.ShapeDtypeStruct((x.shape[1], NANC * 256), F32),
        in_specs=[SMEM, VMEM],
        out_specs=VMEM,
        compiler_params=params(8),
        name="pick_cols",
    )(ancestors, x)


def per_device(sigma_top, factor_cross, factor_inverse, block_inverse, ancestors):
    h, w = sigma_top.shape
    sub = h // 24
    at, at_turned = places(False), places(True)

    f = pick_rows(ancestors, spread(factor_cross))
    inverse = lax.all_gather(after(factor_inverse, f), ROW, axis=0, tiled=True).reshape(16, w, w)
    f_near, f_far, _ = gather_cols(f, True)

    s = pick_rows(ancestors, spread(after(sigma_top, f)))
    s = lax.all_to_all(after(s, f_near[0]).reshape(16, -1, w), COL, 0, 0, tiled=True)
    s_all = lax.all_gather(pick_cols(ancestors, s), COL, axis=0, tiled=True)

    (acc,) = near_product(at, f_near, inverse, 1, W1)
    u, ut = update_product(at, acc, *f_far, inverse)

    u_near, u_far, u_top = gather_cols(turn(ut), False)
    u_tiles = gather_rows(u.reshape(NANC, sub, w))

    sigma = cross_product(at, after(s_all, u_top), u_tiles)
    sigma_all = lax.all_gather(sigma, ROW, axis=0, tiled=True).reshape(8, w, w)
    acc, rows = near_product(at_turned, u_near, sigma_all, 2, W2, ancestors)
    sigma_child = child_product(at_turned, acc, *u_far, sigma_all, block_inverse)

    return (rows.reshape(h, w), sigma_child)


def solution(mesh):
    fine = Mesh(np.asarray(mesh.devices).reshape(4, 2, 4, 4), ALL)
    tile = P(ROW, COL)
    return jax.shard_map(
        per_device,
        mesh=fine,
        in_specs=(tile, tile, tile, tile, P()),
        out_specs=(tile, tile),
        check_vma=False,
    )
```
